32 devices in a mesh: gx: 2 (over x), gy: 4 (over y, core), gz: 4 (over z).
Axes of the slice: x: 2, y: 2, z: 4, core: 2. Of those that a mesh axis runs over, the one named last changes fastest.
Arguments:
- features: bfloat16 [2, 4, 4, 512, 128], P('gx', 'gy', 'gz'), may hold values from -6 to 6
- positions: float32 [2, 4, 4, 3, 512], P('gx', 'gy', 'gz'), may hold values from 0 to 1
- counts: int32 [2, 4, 4], P('gx', 'gy', 'gz'), may hold values from 256 to 512, as said below
- pair_first: int32 [2, 4, 4, 128, 128], P('gx', 'gy', 'gz'), may hold values from 0 to 511, as said below
- pair_second: int32 [2, 4, 4, 128, 128], P('gx', 'gy', 'gz'), may hold values from 0 to 13823, as said below
- pair_mask: int32 [2, 4, 4, 128, 128], P('gx', 'gy', 'gz'), may hold values from 0 to 1, as said below
- w_centre: bfloat16 [128, 256], replicated, may hold values from -0.5 to 0.5
- w_neighbour: bfloat16 [128, 256], replicated, may hold values from -0.5 to 0.5
- w_charge: bfloat16 [128], replicated, may hold values from -0.5 to 0.5
- w_radial: float32 [8, 256], replicated, may hold values from -3.5 to 3.5
- w_hidden: bfloat16 [256, 256], replicated, may hold values from -0.375 to 0.375
- w_energy: float32 [256], replicated, may hold values from -0.375 to 0.375
Outputs:
- forces: float32 [2, 4, 4, 3, 512], P('gx', 'gy', 'gz')
- charge_grad: float32 [2, 4, 4, 512], P('gx', 'gy', 'gz')
The draws below stay inside these ranges and needn't reach their ends.
Inputs may be any that keep to these rules, and one draw needn't show every extreme that they name: `counts`: every brick holds at least half of its slots; some brick is full and some holds exactly half; the atoms present fill the lowest slots. `pair_first`: every listed pair names a present atom of its own brick. `pair_second`: every listed pair names a present atom of the image brick of its slot s (entry s * 512 + a); within slot 13 it differs from the pair's first atom. `pair_mask`: on every brick the tiles that hold a valid pair come before those that hold none; tile 0 always holds valid pairs.
All inputs are finite; a program needn't handle non-finite values.
Results may differ from the reference program's by a relative error of at most 0.0032.
Values may be sent and summed in bfloat16 or wider, within the bound.
A program may use at most 64 MiB of HBM per device.

```python
import jax
import jax.numpy as jnp
from jax import lax

ATOMS = 512
FEAT = 128
HID = 256
RBF = 8
TILES = 128
BX = 2
BY = 4
BZ = 4


def brick_counts(key):
    bricks = BX * BY * BZ
    base_sizes = jax.random.randint(jax.random.fold_in(key, 11), (bricks,), ATOMS // 2, ATOMS + 1)
    chosen = jax.random.randint(jax.random.fold_in(key, 12), (), 0, bricks)
    second = (chosen + 1 + jax.random.randint(jax.random.fold_in(key, 13), (), 0, bricks - 1)) % bricks
    brick_ids = jnp.arange(bricks)
    base_sizes = jnp.where(brick_ids == chosen, ATOMS, base_sizes)
    base_sizes = jnp.where(brick_ids == second, ATOMS // 2, base_sizes)
    return base_sizes.astype(jnp.int32)


def draw_counts(key, part):
    return brick_counts(key).reshape(BX, BY, BZ)


def pair_tables(key):
    bricks = BX * BY * BZ
    sizes_all = brick_counts(key)
    brick_ids = jnp.arange(bricks)[:, None, None]
    coord_x = brick_ids // (BY * BZ)
    coord_y = brick_ids // BZ % BY
    coord_z = brick_ids % BZ
    tile_shape = (bricks, TILES, 128)
    slot_pick = jax.random.randint(jax.random.fold_in(key, 21), tile_shape, 0, 27)
    step_x = slot_pick // 9 - 1
    step_y = slot_pick // 3 % 3 - 1
    step_z = slot_pick % 3 - 1
    other_id = (coord_x + step_x) % BX * (BY * BZ) + (coord_y + step_y) % BY * BZ + (coord_z + step_z) % BZ
    own_size = sizes_all[brick_ids]
    other_size = sizes_all[other_id]
    first_pick = jax.random.randint(jax.random.fold_in(key, 22), tile_shape, 0, 1 << 30) % own_size
    second_draw = jax.random.randint(jax.random.fold_in(key, 23), tile_shape, 0, 1 << 30)
    self_atom = (first_pick + 1 + second_draw % (own_size - 1)) % own_size
    second_atom = jnp.where(slot_pick == 13, self_atom, second_draw % other_size)
    second = slot_pick * ATOMS + second_atom
    lane_id = jnp.arange(128)[None, None, :]
    tile_id = jnp.arange(TILES)[None, :, None]
    corner = (coord_x + 1) % BX * (BY * BZ) + (coord_y + 1) % BY * BZ + (coord_z + 1) % BZ
    head_zero = (tile_id == 0) & (lane_id == 0)
    head_one = (tile_id == 0) & (lane_id == 1)
    first_pick = jnp.where(head_zero, own_size - 1, jnp.where(head_one, 0, first_pick))
    second = jnp.where(head_zero, 26 * ATOMS + sizes_all[corner] - 1, jnp.where(head_one, 0, second))
    live_tiles = jax.random.randint(jax.random.fold_in(key, 24), (bricks,), TILES // 8, TILES + 1)
    full_brick = jax.random.randint(jax.random.fold_in(key, 25), (), 0, bricks)
    live_tiles = jnp.where(jnp.arange(bricks) == full_brick, TILES, live_tiles)
    lanes_on = (jax.random.randint(jax.random.fold_in(key, 26), tile_shape, 0, 8) != 0) | (lane_id < 2)
    mask_out = ((tile_id < live_tiles[:, None, None]) & lanes_on).astype(jnp.int32)
    final_shape = (BX, BY, BZ, TILES, 128)
    return (first_pick.astype(jnp.int32).reshape(final_shape), second.astype(jnp.int32).reshape(final_shape), mask_out.reshape(final_shape))


def draw_pair_first(key, part):
    return pair_tables(key)[0]


def draw_pair_second(key, part):
    return pair_tables(key)[1]


def draw_pair_mask(key, part):
    return pair_tables(key)[2]


def shard_levels(rng, dims, cuts, least, high):
    level, own = 1.0, jax.random.fold_in(rng, 6)
    for position, blocks in cuts:
        heights = jnp.exp(jax.random.uniform(jax.random.fold_in(own, position), (blocks,), jnp.float32, least / len(cuts), high / len(cuts)))
        level = level * jnp.repeat(heights, dims[position] // blocks).reshape([-1 if axis == position else 1 for axis in range(len(dims))])
    return level


def normal_values(own_key, shape, width, reach, shards=(), kind=jnp.bfloat16):
    entries = width * jax.random.normal(own_key, shape, jnp.float32)
    if shards:
        entries = entries * shard_levels(own_key, shape, shards, -0.22, 0.18)
    return jnp.clip(entries, -reach, reach).astype(kind)


def setup_inputs(seed: int = 0) -> dict:
    streams_of = jax.random.split(jax.random.key(seed), 13)
    features = normal_values(streams_of[0], (BX, BY, BZ, ATOMS, FEAT), 1.0, 6.0, ((0, 2), (1, 4), (2, 4)))
    positions = jnp.clip(1.0 * jax.random.uniform(streams_of[1], (BX, BY, BZ, 3, ATOMS), jnp.float32) ** shard_levels(streams_of[1], (BX, BY, BZ, 3, ATOMS), ((0, 2), (1, 4), (2, 4)), -0.2, 0.2), 0.0, 1.0)
    counts = draw_counts(jax.random.fold_in(streams_of[12], 71), 0)
    pair_first = draw_pair_first(jax.random.fold_in(streams_of[12], 71), 0)
    pair_second = draw_pair_second(jax.random.fold_in(streams_of[12], 71), 0)
    pair_mask = draw_pair_mask(jax.random.fold_in(streams_of[12], 71), 0)
    w_centre = normal_values(streams_of[6], (FEAT, HID), FEAT ** -0.5, 0.5)
    w_neighbour = normal_values(streams_of[7], (FEAT, HID), FEAT ** -0.5, 0.5)
    w_charge = normal_values(streams_of[8], (FEAT,), FEAT ** -0.5, 0.5)
    w_radial = normal_values(streams_of[9], (RBF, HID), 3 ** -0.5, 3.5, (), jnp.float32)
    w_hidden = normal_values(streams_of[10], (HID, HID), HID ** -0.5, 0.375)
    w_energy = normal_values(streams_of[11], (HID,), HID ** -0.5, 0.375, (), jnp.float32)
    return dict(features=features, positions=positions, counts=counts, pair_first=pair_first, pair_second=pair_second, pair_mask=pair_mask, w_centre=w_centre, w_neighbour=w_neighbour, w_charge=w_charge, w_radial=w_radial, w_hidden=w_hidden, w_energy=w_energy)


delta_sq = 0.04
spread = 0.3
coulomb = 0.2
root_pi = 1.7724538509055159
block_tiles = 8

def silu_parts(value):
    logistic = jax.nn.sigmoid(value)
    return (value * logistic, logistic * (1.0 + value * (1.0 - logistic)))

def shifted_coords(neighbours):
    steps_axis = jnp.arange(3, dtype=jnp.float32) - 1.0
    zero_grid = jnp.zeros((3, 3, 3), jnp.float32)
    shift_grid = jnp.stack([steps_axis[:, None, None] + zero_grid, steps_axis[None, :, None] + zero_grid, steps_axis[None, None, :] + zero_grid, zero_grid], axis=3)
    moved_grid = neighbours + shift_grid[..., None]
    return jnp.moveaxis(moved_grid, 3, 0).reshape(4, -1)

def pair_block(centre_proj, image_proj, coords_own, coords_all, pick_first, pick_second, pick_mask, w_radial, w_hidden, w_energy):
    rows_i = pick_first.reshape(-1)
    rows_j = pick_second.reshape(-1)
    weight = pick_mask.reshape(-1).astype(jnp.float32)
    place_i = coords_own[:3][:, rows_i]
    place_j = coords_all[:3][:, rows_j]
    charge_i = coords_own[3][rows_i]
    charge_j = coords_all[3][rows_j]
    separation = place_j - place_i
    dist_sq = lax.optimization_barrier(jnp.sum(separation * separation, axis=0)) + delta_sq
    distance = jnp.sqrt(dist_sq)
    centres = 0.25 + 0.3 * jnp.arange(w_radial.shape[0], dtype=jnp.float32)
    offset = distance[None, :] - centres[:, None]
    radial_basis = jnp.exp(-(offset / spread) * (offset / spread))
    radial = lax.dot_general(radial_basis, w_radial, (((0,), (0,)), ((), ())), precision=lax.Precision.HIGHEST)
    pre_one = centre_proj[rows_i].astype(jnp.float32) + image_proj[rows_j].astype(jnp.float32) + radial
    act_one, slope_one = silu_parts(pre_one)
    hidden = act_one.astype(jnp.bfloat16)
    pre_two = jnp.dot(hidden, w_hidden, preferred_element_type=jnp.float32)
    act_two, slope_two = silu_parts(pre_two)
    envelope = jnp.exp(-0.5 * dist_sq)
    readout = jnp.dot(act_two, w_energy, precision=lax.Precision.HIGHEST)
    back_two = (envelope[:, None] * w_energy[None, :] * slope_two).astype(jnp.bfloat16)
    back_one = lax.dot_general(back_two, w_hidden, (((1,), (1,)), ((), ())), preferred_element_type=jnp.float32) * slope_one
    back_basis = lax.dot_general(w_radial, back_one, (((1,), (1,)), ((), ())), precision=lax.Precision.HIGHEST)
    slope_nn = lax.optimization_barrier(jnp.sum(back_basis * radial_basis * (-2.0 * offset / (spread * spread)), axis=0)) - readout * distance * envelope
    screened = lax.erfc(distance)
    coulomb_pot = screened / distance
    slope_coul = -(2.0 / root_pi) * jnp.exp(-dist_sq) / distance - screened / dist_sq
    slope_all = weight * (slope_nn + coulomb * charge_i * charge_j * slope_coul)
    push_pair = separation * (slope_all / distance)[None, :]
    term_i = jnp.concatenate([push_pair, (weight * coulomb * charge_j * coulomb_pot)[None, :]], axis=0)
    term_j = jnp.concatenate([-push_pair, (weight * coulomb * charge_i * coulomb_pot)[None, :]], axis=0)
    return (rows_i, term_i, rows_j, term_j)

def brick_sum(centre_proj, image_proj, coords_own, coords_all, pair_first, pair_second, pair_mask, w_radial, w_hidden, w_energy, block_count):
    atom_slots = centre_proj.shape[0]

    def advance(index, summed):
        begin_row = index * block_tiles
        rows_i, term_i, rows_j, term_j = pair_block(centre_proj, image_proj, coords_own, coords_all, lax.dynamic_slice_in_dim(pair_first, begin_row, block_tiles, 0), lax.dynamic_slice_in_dim(pair_second, begin_row, block_tiles, 0), lax.dynamic_slice_in_dim(pair_mask, begin_row, block_tiles, 0), w_radial, w_hidden, w_energy)
        summed = summed.at[13, :, rows_i].add(term_i.T)
        summed = summed.at[rows_j // atom_slots, :, rows_j % atom_slots].add(term_j.T)
        return summed
    start_sum = jnp.zeros((27, 4, atom_slots), jnp.float32)
    return lax.fori_loop(0, block_count, advance, start_sum)

def reference(features, positions, counts, pair_first, pair_second, pair_mask, w_centre, w_neighbour, w_charge, w_radial, w_hidden, w_energy):
    raw_charge = jnp.dot(features, w_charge, preferred_element_type=jnp.float32)
    slot_index = jnp.arange(ATOMS, dtype=jnp.int32)
    alive_slot = slot_index[None, None, None, :] < counts[..., None]
    average = lax.optimization_barrier(jnp.sum(jnp.where(alive_slot, raw_charge, 0.0), axis=-1)) / counts.astype(jnp.float32)
    charges = jnp.where(alive_slot, raw_charge - average[..., None], 0.0)
    coords = jnp.concatenate([positions, charges[:, :, :, None, :]], axis=3)
    centre_all = jnp.dot(features, w_centre, preferred_element_type=jnp.float32).astype(jnp.bfloat16)
    image_all = jnp.dot(features, w_neighbour, preferred_element_type=jnp.float32).astype(jnp.bfloat16)
    three = jnp.arange(3, dtype=jnp.int32) - 1

    def per_brick(brick_id):
        coord_x = brick_id // (BY * BZ)
        coord_y = brick_id // BZ % BY
        coord_z = brick_id % BZ
        near_x = (coord_x + three) % BX
        near_y = (coord_y + three) % BY
        near_z = (coord_z + three) % BZ

        def beside_all(table_all):
            return jnp.take(jnp.take(jnp.take(table_all, near_x, axis=0), near_y, axis=1), near_z, axis=2)
        image_proj = beside_all(image_all).reshape(27 * ATOMS, HID)
        coords_all = shifted_coords(beside_all(coords))
        return brick_sum(centre_all[coord_x, coord_y, coord_z], image_proj, coords[coord_x, coord_y, coord_z], coords_all, pair_first[coord_x, coord_y, coord_z], pair_second[coord_x, coord_y, coord_z], pair_mask[coord_x, coord_y, coord_z], w_radial, w_hidden, w_energy, TILES // block_tiles)
    partial_all = lax.map(per_brick, jnp.arange(BX * BY * BZ, dtype=jnp.int32))
    partial_all = partial_all.reshape(BX, BY, BZ, 3, 3, 3, 4, ATOMS)
    summed = jnp.zeros((BX, BY, BZ, 4, ATOMS), jnp.float32)
    for step_x in range(3):
        for step_y in range(3):
            for step_z in range(3):
                summed = summed + jnp.roll(partial_all[:, :, :, step_x, step_y, step_z], (step_x - 1, step_y - 1, step_z - 1), axis=(0, 1, 2))
    return (summed[:, :, :, :3], summed[:, :, :, 3])
```

```python
import functools

import jax
import jax.numpy as jnp
from jax import lax
from jax.experimental import pallas as pl
from jax.experimental.pallas import tpu as pltpu
from jax.sharding import PartitionSpec as P

delta_sq = 0.04
spread = 0.3
coulomb = 0.2
root_pi = 1.7724538509055159
part_rows = 16
erfc_terms = (
    0.17087277,
    -0.82215223,
    1.48851587,
    -1.13520398,
    0.27886807,
    -0.18628806,
    0.09678418,
    0.37409196,
    1.00002368,
    -1.26551223,
)


def ring(axis, step):
    count = lax.axis_size(axis)
    return [(i, (i + step) % count) for i in range(count)]


def widen(block, axis):
    parts = [block, lax.ppermute(block, axis, ring(axis, -1))]
    if lax.axis_size(axis) > 2:
        parts.append(lax.ppermute(block, axis, ring(axis, 1)))
    return parts


def fold(blocks, axis):
    total = blocks[0] + lax.ppermute(blocks[1], axis, ring(axis, 1))
    if len(blocks) > 2:
        total = total + lax.ppermute(blocks[2], axis, ring(axis, -1))
    return total


def rounded(value):
    return lax.reduce_precision(value, 8, 7)


def three_parts(value):
    high = rounded(value)
    middle = rounded(value - high)
    return [high, middle, rounded(value - high - middle)]


def lower(left, right):
    return jnp.dot(left, right, preferred_element_type=jnp.float32)


def pair_kernel(
    width,
    plan_ref,
    pairs_ref,
    *refs,
):
    (
        *table_refs,
        to_centre_ref,
        to_image_ref,
        radial_cat_ref,
        radial_two_ref,
        hidden_ref,
        hidden_t_ref,
        energy_ref,
        out_ref,
        centre_ref,
        image_ref,
        pre_ref,
        sum_i_ref,
        sum_j_ref,
    ) = refs
    atoms = centre_ref.shape[1]
    lanes = pairs_ref.shape[2]
    hid = hidden_ref.shape[0]
    cuts = atoms // width

    centre_ref[...] = lower(to_centre_ref[...], table_refs[0][0]).astype(jnp.bfloat16)
    begin = 0
    for table_ref in table_refs:
        def project(index, carry, table_ref=table_ref, begin=begin):
            image = lower(to_image_ref[...], table_ref[index]).astype(jnp.bfloat16)
            for cut in range(cuts):
                image_ref[(begin + index) * cuts + cut] = image[:, cut * width : (cut + 1) * width]
            return carry

        lax.fori_loop(0, table_ref.shape[0], project, 0)
        begin += table_ref.shape[0]
    sum_i_ref[...] = jnp.zeros_like(sum_i_ref)
    sum_j_ref[...] = jnp.zeros_like(sum_j_ref)

    def pick(rows, entries):
        spot = lax.broadcasted_iota(jnp.int32, (rows, lanes), 0)
        return jnp.where(spot == entries, 1.0, 0.0).astype(jnp.bfloat16)

    def step(block, carry):
        listed = pairs_ref[block]
        first = listed[0:1]
        second = listed[1:2]
        offset_x = listed[2:3].astype(jnp.float32)
        offset_y = listed[3:4].astype(jnp.float32)
        offset_z = listed[4:5].astype(jnp.float32)
        weight = listed[5:6].astype(jnp.float32)
        least = plan_ref[2 * block + 1]
        most = plan_ref[2 * block + 2]
        pick_i = pick(atoms, first)
        pre_ref[...] = lower(centre_ref[...], pick_i)

        def gather(window, carry):
            pre_ref[...] += lower(image_ref[window], pick(width, second - window * width))
            return carry

        lax.fori_loop(least, most + 1, gather, 0)
        extra = pre_ref[hid:, :]
        sep_x = (extra[0:1] + extra[3:4]) + extra[6:7] + offset_x
        sep_y = (extra[1:2] + extra[4:5]) + extra[7:8] + offset_y
        sep_z = (extra[2:3] + extra[5:6]) + extra[8:9] + offset_z
        charge_i = extra[9:10] + extra[10:11] + extra[11:12]
        charge_j = extra[12:13] + extra[13:14] + extra[14:15]
        dist_sq = sep_x * sep_x + sep_y * sep_y + sep_z * sep_z + delta_sq
        distance = jnp.sqrt(dist_sq)
        inverse = 1.0 / distance
        envelope = jnp.exp(-0.5 * dist_sq)
        basis_count = radial_two_ref.shape[0] // 2
        order = lax.broadcasted_iota(jnp.int32, (basis_count, lanes), 0).astype(jnp.float32)
        offset = distance - (0.25 + 0.3 * order)
        basis = jnp.exp(-(offset / spread) * (offset / spread))
        basis_high = basis.astype(jnp.bfloat16).astype(jnp.float32)
        basis_cat = jnp.concatenate(
            [basis_high, basis - basis_high, basis_high, jnp.zeros_like(basis)], axis=0
        ).astype(jnp.bfloat16)
        pre_one = pre_ref[:hid, :] + lower(radial_cat_ref[...], basis_cat)
        gate_one = 0.5 * jnp.tanh(0.5 * pre_one) + 0.5
        act_one = pre_one * gate_one
        slope_one = gate_one + act_one * (1.0 - gate_one)
        pre_two = lower(hidden_t_ref[...], act_one.astype(jnp.bfloat16))
        gate_two = 0.5 * jnp.tanh(0.5 * pre_two) + 0.5
        scaled = energy_ref[...] * gate_two
        scaled_act = pre_two * scaled
        readout = jnp.sum(scaled_act, axis=0, keepdims=True)
        back_two = (envelope * (scaled + scaled_act * (1.0 - gate_two))).astype(jnp.bfloat16)
        back_one = lower(hidden_ref[...], back_two) * slope_one
        back_high = back_one.astype(jnp.bfloat16)
        back_low = (back_one - back_high.astype(jnp.float32)).astype(jnp.bfloat16)
        from_high = lower(radial_two_ref[...], back_high)
        from_low = lower(radial_two_ref[...], back_low)
        back_basis = from_high[:basis_count] + from_high[basis_count:] + from_low[:basis_count]
        slope_nn = (
            jnp.sum(
                back_basis * basis * (offset * (-2.0 / (spread * spread))), axis=0, keepdims=True
            )
            - readout * distance * envelope
        )
        ratio = 1.0 / (1.0 + 0.5 * distance)
        series = jnp.full_like(ratio, erfc_terms[0])
        for term in erfc_terms[1:]:
            series = series * ratio + term
        screened = ratio * jnp.exp(series - distance * distance)
        potential = screened * inverse
        slope_coul = -(2.0 / root_pi) * jnp.exp(-dist_sq) * inverse - potential * inverse
        slope = weight * (slope_nn + coulomb * charge_i * charge_j * slope_coul) * inverse
        push_x = slope * sep_x
        push_y = slope * sep_y
        push_z = slope * sep_z
        shared = weight * coulomb * potential
        terms = jnp.concatenate(
            [
                push_x,
                push_y,
                push_z,
                shared * charge_j,
                -push_x,
                -push_y,
                -push_z,
                shared * charge_i,
            ],
            axis=0,
        )
        terms_high = terms.astype(jnp.bfloat16).astype(jnp.float32)
        both = jnp.concatenate([terms_high, terms - terms_high], axis=0).astype(jnp.bfloat16)
        across = (((1,), (1,)), ((), ()))
        sum_i_ref[...] += lax.dot_general(
            both, pick_i, across, preferred_element_type=jnp.float32
        )

        def scatter(window, carry):
            sum_j_ref[window] += lax.dot_general(
                both,
                pick(width, second - window * width),
                across,
                preferred_element_type=jnp.float32,
            )
            return carry

        lax.fori_loop(least, most + 1, scatter, 0)
        return carry

    lax.fori_loop(0, plan_ref[0], step, 0)

    def finish(index, carry):
        for cut in range(cuts):
            total = sum_j_ref[index * cuts + cut]
            out_ref[index, :, cut * width : (cut + 1) * width] = total[4:8] + total[12:16]
        return carry

    lax.fori_loop(0, out_ref.shape[0], finish, 0)
    out_ref[0] += sum_i_ref[0:4, :] + sum_i_ref[8:12, :]


def local(
    features,
    positions,
    counts,
    pair_first,
    pair_second,
    pair_mask,
    w_centre,
    w_neighbour,
    w_charge,
    w_radial,
    w_hidden,
    w_energy,
):
    own_feat = features[0, 0, 0]
    atoms, feat = own_feat.shape
    hid = w_hidden.shape[0]
    spans = [min(3, lax.axis_size(axis)) for axis in ("gx", "gy", "gz")]
    raw_charge = jnp.dot(own_feat, w_charge, preferred_element_type=jnp.float32)
    filled = counts[0, 0, 0]
    alive_slot = jnp.arange(atoms, dtype=jnp.int32) < filled
    average = jnp.sum(jnp.where(alive_slot, raw_charge, 0.0)) / filled.astype(jnp.float32)
    charges = jnp.where(alive_slot, raw_charge - average, 0.0)
    own = jnp.concatenate(
        three_parts(positions[0, 0, 0])
        + three_parts(charges[None, :])
        + [jnp.zeros((part_rows - 12, atoms), jnp.float32)],
        axis=0,
    ).astype(jnp.bfloat16)
    own = jnp.concatenate([own_feat.T, own], axis=0)

    column = jnp.stack(widen(own, "gz"))
    plane = jnp.concatenate(widen(column, "gx"))
    tables = widen(plane, "gy")

    entry = pair_second[0, 0, 0].reshape(-1)
    slot = entry // atoms
    steps = (slot // 9 - 1, slot // 3 % 3 - 1, slot % 3 - 1)
    place = [jnp.where(step < 0, span - 1, step) for step, span in zip(steps, spans)]
    brick = (place[1] * spans[0] + place[0]) * spans[2] + place[2]
    bricks = spans[0] * spans[1] * spans[2]
    sign = ((steps[0] + 1) * 3 + steps[1] + 1) * 3 + steps[2] + 1
    key = ((brick * atoms + entry % atoms) * atoms + pair_first[0, 0, 0].reshape(-1)) * 27 + sign
    mask = pair_mask[0, 0, 0].reshape(-1) != 0
    key = jnp.where(mask, key, bricks * atoms * atoms * 27)
    key = lax.sort(key, is_stable=False)
    valid = jnp.sum(mask.astype(jnp.int32))
    lanes = 512 if key.shape[0] % 512 == 0 else 128
    width = 256 if atoms % 256 == 0 else 128
    blocks = key.shape[0] // lanes
    key = key.reshape(blocks, lanes)
    sign = key % 27
    second = key // (27 * atoms)
    rows = [
        key // 27 % atoms,
        second,
        sign // 9 - 1,
        sign // 3 % 3 - 1,
        sign % 3 - 1,
        (second < bricks * atoms).astype(jnp.int32),
    ]
    rows = rows + [jnp.zeros_like(key)] * 2
    listed = jnp.stack(rows, axis=1)
    window = jnp.minimum(second // width, bricks * atoms // width - 1)
    live = (valid + lanes - 1) // lanes
    plan = jnp.concatenate(
        [live[None], jnp.stack([window[:, 0], jnp.max(window, axis=1)], axis=1).reshape(-1)]
    ).astype(jnp.int32)

    carry_j = [[0.0] * part_rows for _ in range(part_rows)]
    carry_i = [[0.0] * part_rows for _ in range(part_rows)]
    for part in range(9):
        carry_j[part][part] = 1.0
        carry_i[part][part] = -1.0
    for part in range(3):
        carry_i[9 + part][9 + part] = 1.0
        carry_j[12 + part][9 + part] = 1.0

    def with_parts(weight, carried):
        top = jnp.concatenate([weight.T, jnp.zeros((hid, part_rows), jnp.bfloat16)], axis=1)
        bottom = jnp.concatenate(
            [jnp.zeros((part_rows, feat), jnp.bfloat16), jnp.array(carried, jnp.bfloat16)], axis=1
        )
        return jnp.concatenate([top, bottom], axis=0)

    radial_high = rounded(w_radial)
    radial_low = w_radial - radial_high
    radial_cat = jnp.concatenate(
        [radial_high, radial_high, radial_low, jnp.zeros_like(w_radial)], axis=0
    ).T.astype(jnp.bfloat16)
    radial_two = jnp.concatenate([radial_high, radial_low], axis=0).astype(jnp.bfloat16)

    vmem = pl.BlockSpec(memory_space=pltpu.VMEM)
    operands = [listed, *tables]
    operands += [with_parts(w_centre, carry_i), with_parts(w_neighbour, carry_j)]
    operands += [radial_cat, radial_two, w_hidden, w_hidden.T, w_energy[:, None]]
    windows = bricks * atoms // width
    partial = pl.pallas_call(
        functools.partial(pair_kernel, width),
        out_shape=jax.ShapeDtypeStruct((bricks, 4, atoms), jnp.float32),
        in_specs=[pl.BlockSpec(memory_space=pltpu.SMEM)] + [vmem] * len(operands),
        out_specs=vmem,
        scratch_shapes=[
            pltpu.VMEM((hid + part_rows, atoms), jnp.bfloat16),
            pltpu.VMEM((windows, hid + part_rows, width), jnp.bfloat16),
            pltpu.VMEM((hid + part_rows, lanes), jnp.float32),
            pltpu.VMEM((16, atoms), jnp.float32),
            pltpu.VMEM((windows, 16, width), jnp.float32),
        ],
        compiler_params=pltpu.CompilerParams(vmem_limit_bytes=48 * 1024 * 1024),
        name="pairs",
    )(plan, *operands)
    partial = partial.reshape(spans[1], spans[0], spans[2], 4, atoms)
    partial = fold(partial, "gy")
    partial = fold(partial, "gx")
    summed = fold(partial, "gz")
    return (summed[:3][None, None, None], summed[3][None, None, None])


def solution(mesh):
    placed = (
        P("gx", "gy", "gz", None, None),
        P("gx", "gy", "gz", None, None),
        P("gx", "gy", "gz"),
        P("gx", "gy", "gz", None, None),
        P("gx", "gy", "gz", None, None),
        P("gx", "gy", "gz", None, None),
        P(),
        P(),
        P(),
        P(),
        P(),
        P(),
    )
    return jax.shard_map(
        local,
        mesh=mesh,
        in_specs=placed,
        out_specs=(P("gx", "gy", "gz", None, None), P("gx", "gy", "gz", None)),
        check_vma=False,
    )
```

```python
import functools

import jax
import jax.numpy as jnp
from jax import lax
from jax.experimental import pallas as pl
from jax.experimental.pallas import tpu as pltpu
from jax.sharding import PartitionSpec as P

delta_sq = 0.04
spread = 0.3
coulomb = 0.2
root_pi = 1.7724538509055159
part_rows = 16
subs = 2
erfc_terms = (
    0.17087277,
    -0.82215223,
    1.48851587,
    -1.13520398,
    0.27886807,
    -0.18628806,
    0.09678418,
    0.37409196,
    1.00002368,
    -1.26551223,
)


def ring(axis, step):
    count = lax.axis_size(axis)
    return [(i, (i + step) % count) for i in range(count)]


def widen(block, axis):
    parts = [block, lax.ppermute(block, axis, ring(axis, -1))]
    if lax.axis_size(axis) > 2:
        parts.append(lax.ppermute(block, axis, ring(axis, 1)))
    return parts


def fold(blocks, axis):
    total = blocks[0] + lax.ppermute(blocks[1], axis, ring(axis, 1))
    if len(blocks) > 2:
        total = total + lax.ppermute(blocks[2], axis, ring(axis, -1))
    return total


def rounded(value):
    return lax.reduce_precision(value, 8, 7)


def three_parts(value):
    high = rounded(value)
    middle = rounded(value - high)
    return [high, middle, rounded(value - high - middle)]


def lower(left, right):
    return jnp.dot(left, right, preferred_element_type=jnp.float32)


def pair_kernel(
    width,
    plan_ref,
    pairs_ref,
    *refs,
):
    (
        *table_refs,
        to_centre_ref,
        to_image_ref,
        radial_cat_ref,
        radial_two_ref,
        hidden_ref,
        hidden_t_ref,
        energy_ref,
        out_ref,
        centre_ref,
        image_ref,
        pre_ref,
        sum_i_ref,
        sum_j_ref,
        pick_i_ref,
        pick_j_ref,
        terms_ref,
    ) = refs
    basis_count = radial_two_ref.shape[0] // 2
    atoms = centre_ref.shape[1]
    lanes = pairs_ref.shape[2]
    hid = hidden_ref.shape[0]
    cuts = atoms // width

    centre_ref[...] = lower(to_centre_ref[...], table_refs[0][0]).astype(jnp.bfloat16)
    begin = 0
    for table_ref in table_refs:
        def project(index, carry, table_ref=table_ref, begin=begin):
            image = lower(to_image_ref[...], table_ref[index]).astype(jnp.bfloat16)
            for cut in range(cuts):
                image_ref[(begin + index) * cuts + cut] = image[:, cut * width : (cut + 1) * width]
            return carry

        lax.fori_loop(0, table_ref.shape[0], project, 0)
        begin += table_ref.shape[0]
    sum_i_ref[...] = jnp.zeros_like(sum_i_ref)
    sum_j_ref[...] = jnp.zeros_like(sum_j_ref)

    chunk = 16
    ladder = lax.broadcasted_iota(jnp.int32, (chunk, lanes), 0).astype(jnp.int16)

    def pick(rows, entries):
        spread_out = jnp.broadcast_to(entries, (chunk, lanes)).astype(jnp.int16)
        one = jnp.ones((chunk, lanes), jnp.bfloat16)
        zero = jnp.zeros((chunk, lanes), jnp.bfloat16)
        return jnp.concatenate(
            [
                jnp.where(spread_out == ladder + jnp.int16(base), one, zero)
                for base in range(0, rows, chunk)
            ],
            axis=0,
        )

    across = (((1,), (1,)), ((), ()))

    def spill(terms, picked):
        return lax.dot_general(terms, picked, across, preferred_element_type=jnp.float32)

    def begin_part(part):
        listed = pairs_ref[part]
        least = plan_ref[2 * part + 1]
        after = jnp.minimum(least + 1, image_ref.shape[0] - 1)
        pick_i = pick(atoms, listed[0:1])
        pick_j = pick(2 * width, listed[1:2] - least * width)
        pre = lower(centre_ref[...], pick_i)
        pre += lower(image_ref[least], pick_j[:width])
        pre += lower(image_ref[after], pick_j[width:])
        return pre, pick_i, pick_j

    def geometry(part, lane):
        listed = pairs_ref[part]
        extra = pre_ref[lane, hid:, :]
        sep_x = (extra[0:1] + extra[3:4]) + extra[6:7] + listed[2:3].astype(jnp.float32)
        sep_y = (extra[1:2] + extra[4:5]) + extra[7:8] + listed[3:4].astype(jnp.float32)
        sep_z = (extra[2:3] + extra[5:6]) + extra[8:9] + listed[4:5].astype(jnp.float32)
        dist_sq = sep_x * sep_x + sep_y * sep_y + sep_z * sep_z + delta_sq
        distance = jnp.sqrt(dist_sq)
        order = lax.broadcasted_iota(jnp.int32, (basis_count, lanes), 0).astype(jnp.float32)
        offset = distance - (0.25 + 0.3 * order)
        basis = jnp.exp(-(offset / spread) * (offset / spread))
        basis_high = basis.astype(jnp.bfloat16).astype(jnp.float32)
        basis_cat = jnp.concatenate(
            [basis_high, basis - basis_high, basis_high, jnp.zeros_like(basis)], axis=0
        ).astype(jnp.bfloat16)
        pre_one = pre_ref[lane, :hid, :] + lower(radial_cat_ref[...], basis_cat)
        return (sep_x, sep_y, sep_z), dist_sq, distance, offset, basis, pre_one

    def first_layer(pre_one):
        gate = 0.5 * jnp.tanh(0.5 * pre_one) + 0.5
        act = pre_one * gate
        return act.astype(jnp.bfloat16), gate + act * (1.0 - gate)

    def second_layer(pre_two, dist_sq):
        gate = 0.5 * jnp.tanh(0.5 * pre_two) + 0.5
        scaled = energy_ref[...] * gate
        scaled_act = pre_two * scaled
        readout = jnp.sum(scaled_act, axis=0, keepdims=True)
        envelope = jnp.exp(-0.5 * dist_sq)
        back = (envelope * (scaled + scaled_act * (1.0 - gate))).astype(jnp.bfloat16)
        return back, readout * envelope

    def pair_terms(part, lane, shape, back_basis, readout):
        (sep_x, sep_y, sep_z), dist_sq, distance, offset, basis, _ = shape
        weight = pairs_ref[part][5:6].astype(jnp.float32)
        extra = pre_ref[lane, hid:, :]
        charge_i = extra[9:10] + extra[10:11] + extra[11:12]
        charge_j = extra[12:13] + extra[13:14] + extra[14:15]
        inverse = 1.0 / distance
        slope_nn = (
            jnp.sum(
                back_basis * basis * (offset * (-2.0 / (spread * spread))), axis=0, keepdims=True
            )
            - readout * distance
        )
        ratio = 1.0 / (1.0 + 0.5 * distance)
        series = jnp.full_like(ratio, erfc_terms[0])
        for term in erfc_terms[1:]:
            series = series * ratio + term
        screened = ratio * jnp.exp(series - distance * distance)
        potential = screened * inverse
        slope_coul = -(2.0 / root_pi) * jnp.exp(-dist_sq) * inverse - potential * inverse
        slope = weight * (slope_nn + coulomb * charge_i * charge_j * slope_coul) * inverse
        push_x = slope * sep_x
        push_y = slope * sep_y
        push_z = slope * sep_z
        shared = weight * coulomb * potential
        terms = jnp.concatenate(
            [
                push_x,
                push_y,
                push_z,
                shared * charge_j,
                -push_x,
                -push_y,
                -push_z,
                shared * charge_i,
            ],
            axis=0,
        )
        terms_high = terms.astype(jnp.bfloat16).astype(jnp.float32)
        return jnp.concatenate([terms_high, terms - terms_high], axis=0).astype(jnp.bfloat16)

    def step(block, carry):
        parts = [block * subs + lane for lane in range(subs)]
        for lane, part in enumerate(parts):
            pre, pick_i, pick_j = begin_part(part)
            pre_ref[lane] = pre
            pick_i_ref[lane] = pick_i
            pick_j_ref[lane] = pick_j

        for lane, part in enumerate(parts):
            def gather(window, carry, lane=lane, part=part):
                entries = pairs_ref[part][1:2] - window * width
                pre_ref[lane] += lower(image_ref[window], pick(width, entries))
                return carry

            lax.fori_loop(plan_ref[2 * part + 1] + 2, plan_ref[2 * part + 2] + 1, gather, 0)

        shapes = [geometry(part, lane) for lane, part in enumerate(parts)]
        ones = [first_layer(shape[-1]) for shape in shapes]
        twos = [lower(hidden_t_ref[...], one[0]) for one in ones]
        backs = [second_layer(two, shape[1]) for two, shape in zip(twos, shapes)]
        grads = [
            (lower(hidden_ref[...], back[0]) * one[1]).astype(jnp.bfloat16)
            for back, one in zip(backs, ones)
        ]
        for lane, part in enumerate(parts):
            from_grad = lower(radial_two_ref[...], grads[lane])
            back_basis = from_grad[:basis_count] + from_grad[basis_count:]
            terms_ref[lane] = pair_terms(part, lane, shapes[lane], back_basis, backs[lane][1])
        for lane, part in enumerate(parts):
            least = plan_ref[2 * part + 1]
            after = jnp.minimum(least + 1, image_ref.shape[0] - 1)
            terms = terms_ref[lane]
            sum_i_ref[...] += spill(terms, pick_i_ref[lane])
            sum_j_ref[least] += spill(terms, pick_j_ref[lane, :width])
            sum_j_ref[after] += spill(terms, pick_j_ref[lane, width:])

        for lane, part in enumerate(parts):
            def scatter(window, carry, lane=lane, part=part):
                entries = pairs_ref[part][1:2] - window * width
                sum_j_ref[window] += spill(terms_ref[lane], pick(width, entries))
                return carry

            lax.fori_loop(plan_ref[2 * part + 1] + 2, plan_ref[2 * part + 2] + 1, scatter, 0)
        return carry

    lax.fori_loop(0, plan_ref[0], step, 0)

    def finish(index, carry):
        for cut in range(cuts):
            total = sum_j_ref[index * cuts + cut]
            out_ref[index, :, cut * width : (cut + 1) * width] = total[4:8] + total[12:16]
        return carry

    lax.fori_loop(0, out_ref.shape[0], finish, 0)
    out_ref[0] += sum_i_ref[0:4, :] + sum_i_ref[8:12, :]


def local(
    features,
    positions,
    counts,
    pair_first,
    pair_second,
    pair_mask,
    w_centre,
    w_neighbour,
    w_charge,
    w_radial,
    w_hidden,
    w_energy,
):
    own_feat = features[0, 0, 0]
    atoms, feat = own_feat.shape
    hid = w_hidden.shape[0]
    spans = [min(3, lax.axis_size(axis)) for axis in ("gx", "gy", "gz")]
    raw_charge = jnp.dot(own_feat, w_charge, preferred_element_type=jnp.float32)
    filled = counts[0, 0, 0]
    alive_slot = jnp.arange(atoms, dtype=jnp.int32) < filled
    average = jnp.sum(jnp.where(alive_slot, raw_charge, 0.0)) / filled.astype(jnp.float32)
    charges = jnp.where(alive_slot, raw_charge - average, 0.0)
    own = jnp.concatenate(
        three_parts(positions[0, 0, 0])
        + three_parts(charges[None, :])
        + [jnp.zeros((part_rows - 12, atoms), jnp.float32)],
        axis=0,
    ).astype(jnp.bfloat16)
    own = jnp.concatenate([own_feat.T, own], axis=0)

    column = jnp.stack(widen(own, "gz"))
    plane = jnp.concatenate(widen(column, "gx"))
    tables = widen(plane, "gy")

    entry = pair_second[0, 0, 0].reshape(-1)
    slot = entry // atoms
    steps = (slot // 9 - 1, slot // 3 % 3 - 1, slot % 3 - 1)
    place = [jnp.where(step < 0, span - 1, step) for step, span in zip(steps, spans)]
    brick = (place[1] * spans[0] + place[0]) * spans[2] + place[2]
    bricks = spans[0] * spans[1] * spans[2]
    sign = ((steps[0] + 1) * 3 + steps[1] + 1) * 3 + steps[2] + 1
    key = ((brick * atoms + entry % atoms) * atoms + pair_first[0, 0, 0].reshape(-1)) * 27 + sign
    mask = pair_mask[0, 0, 0].reshape(-1) != 0
    key = jnp.where(mask, key, bricks * atoms * atoms * 27)
    key = lax.sort(key, is_stable=False)
    valid = jnp.sum(mask.astype(jnp.int32))
    lanes = 256 if key.shape[0] % (256 * subs) == 0 else 128
    width = 256 if atoms % 256 == 0 else 128
    blocks = key.shape[0] // lanes
    key = key.reshape(blocks, lanes)
    sign = key % 27
    second = key // (27 * atoms)
    rows = [
        key // 27 % atoms,
        second,
        sign // 9 - 1,
        sign // 3 % 3 - 1,
        sign % 3 - 1,
        (second < bricks * atoms).astype(jnp.int32),
    ]
    rows = rows + [jnp.zeros_like(key)] * 2
    listed = jnp.stack(rows, axis=1)
    window = jnp.minimum(second // width, bricks * atoms // width - 1)
    live = (valid + subs * lanes - 1) // (subs * lanes)
    plan = jnp.concatenate(
        [live[None], jnp.stack([window[:, 0], jnp.max(window, axis=1)], axis=1).reshape(-1)]
    ).astype(jnp.int32)

    carry_j = [[0.0] * part_rows for _ in range(part_rows)]
    carry_i = [[0.0] * part_rows for _ in range(part_rows)]
    for part in range(9):
        carry_j[part][part] = 1.0
        carry_i[part][part] = -1.0
    for part in range(3):
        carry_i[9 + part][9 + part] = 1.0
        carry_j[12 + part][9 + part] = 1.0

    def with_parts(weight, carried):
        top = jnp.concatenate([weight.T, jnp.zeros((hid, part_rows), jnp.bfloat16)], axis=1)
        bottom = jnp.concatenate(
            [jnp.zeros((part_rows, feat), jnp.bfloat16), jnp.array(carried, jnp.bfloat16)], axis=1
        )
        return jnp.concatenate([top, bottom], axis=0)

    radial_high = rounded(w_radial)
    radial_low = w_radial - radial_high
    radial_cat = jnp.concatenate(
        [radial_high, radial_high, radial_low, jnp.zeros_like(w_radial)], axis=0
    ).T.astype(jnp.bfloat16)
    radial_two = jnp.concatenate([radial_high, radial_low], axis=0).astype(jnp.bfloat16)

    vmem = pl.BlockSpec(memory_space=pltpu.VMEM)
    operands = [listed, *tables]
    operands += [with_parts(w_centre, carry_i), with_parts(w_neighbour, carry_j)]
    operands += [radial_cat, radial_two, w_hidden, w_hidden.T, w_energy[:, None]]
    windows = bricks * atoms // width
    partial = pl.pallas_call(
        functools.partial(pair_kernel, width),
        out_shape=jax.ShapeDtypeStruct((bricks, 4, atoms), jnp.float32),
        in_specs=[pl.BlockSpec(memory_space=pltpu.SMEM)] + [vmem] * len(operands),
        out_specs=vmem,
        scratch_shapes=[
            pltpu.VMEM((hid + part_rows, atoms), jnp.bfloat16),
            pltpu.VMEM((windows, hid + part_rows, width), jnp.bfloat16),
            pltpu.VMEM((subs, hid + part_rows, lanes), jnp.float32),
            pltpu.VMEM((16, atoms), jnp.float32),
            pltpu.VMEM((windows, 16, width), jnp.float32),
            pltpu.VMEM((subs, atoms, lanes), jnp.bfloat16),
            pltpu.VMEM((subs, 2 * width, lanes), jnp.bfloat16),
            pltpu.VMEM((subs, 16, lanes), jnp.bfloat16),
        ],
        compiler_params=pltpu.CompilerParams(vmem_limit_bytes=48 * 1024 * 1024),
        name="pairs",
    )(plan, *operands)
    partial = partial.reshape(spans[1], spans[0], spans[2], 4, atoms)
    partial = fold(partial, "gy")
    partial = fold(partial, "gx")
    summed = fold(partial, "gz")
    return (summed[:3][None, None, None], summed[3][None, None, None])


def solution(mesh):
    placed = (
        P("gx", "gy", "gz", None, None),
        P("gx", "gy", "gz", None, None),
        P("gx", "gy", "gz"),
        P("gx", "gy", "gz", None, None),
        P("gx", "gy", "gz", None, None),
        P("gx", "gy", "gz", None, None),
        P(),
        P(),
        P(),
        P(),
        P(),
        P(),
    )
    return jax.shard_map(
        local,
        mesh=mesh,
        in_specs=placed,
        out_specs=(P("gx", "gy", "gz", None, None), P("gx", "gy", "gz", None)),
        check_vma=False,
    )
```

```python
import functools

import jax
import jax.numpy as jnp
from jax import lax
from jax.experimental import pallas as pl
from jax.experimental.pallas import tpu as pltpu
from jax.sharding import PartitionSpec as P

delta_sq = 0.04
spread = 0.3
coulomb = 0.2
root_pi = 1.7724538509055159
part_rows = 16
subs = 2
erfc_terms = (
    0.17087277,
    -0.82215223,
    1.48851587,
    -1.13520398,
    0.27886807,
    -0.18628806,
    0.09678418,
    0.37409196,
    1.00002368,
    -1.26551223,
)


def ring(axis, step):
    count = lax.axis_size(axis)
    return [(i, (i + step) % count) for i in range(count)]


def widen(block, axis):
    parts = [block, lax.ppermute(block, axis, ring(axis, -1))]
    if lax.axis_size(axis) > 2:
        parts.append(lax.ppermute(block, axis, ring(axis, 1)))
    return parts


def fold(blocks, axis):
    total = blocks[0] + lax.ppermute(blocks[1], axis, ring(axis, 1))
    if len(blocks) > 2:
        total = total + lax.ppermute(blocks[2], axis, ring(axis, -1))
    return total


def rounded(value):
    return lax.reduce_precision(value, 8, 7)


def three_parts(value):
    high = rounded(value)
    middle = rounded(value - high)
    return [high, middle, rounded(value - high - middle)]


def lower(left, right):
    return jnp.dot(left, right, preferred_element_type=jnp.float32)


def pair_kernel(
    width,
    stage,
    plan_ref,
    pairs_ref,
    *refs,
):
    before_ref = refs[0] if stage else None
    (
        *table_refs,
        to_centre_ref,
        to_image_ref,
        radial_cat_ref,
        radial_two_ref,
        hidden_ref,
        hidden_t_ref,
        energy_ref,
        out_ref,
        centre_ref,
        image_ref,
        pre_ref,
        sum_i_ref,
        sum_j_ref,
        pick_i_ref,
        pick_j_ref,
        terms_ref,
    ) = refs[1:] if stage else refs
    basis_count = radial_two_ref.shape[0] // 2
    atoms = centre_ref.shape[1]
    lanes = pairs_ref.shape[2]
    hid = hidden_ref.shape[0]
    cuts = atoms // width

    centre_ref[...] = lower(to_centre_ref[...], table_refs[0][0]).astype(jnp.bfloat16)
    begin = 0
    for table_ref in table_refs:
        def project(index, carry, table_ref=table_ref, begin=begin):
            image = lower(to_image_ref[...], table_ref[index]).astype(jnp.bfloat16)
            for cut in range(cuts):
                image_ref[(begin + index) * cuts + cut] = image[:, cut * width : (cut + 1) * width]
            return carry

        lax.fori_loop(0, table_ref.shape[0], project, 0)
        begin += table_ref.shape[0]
    sum_i_ref[...] = jnp.zeros_like(sum_i_ref)
    sum_j_ref[...] = jnp.zeros_like(sum_j_ref)

    chunk = 16
    ladder = lax.broadcasted_iota(jnp.int32, (chunk, lanes), 0).astype(jnp.int16)

    def pick(rows, entries):
        spread_out = jnp.broadcast_to(entries, (chunk, lanes)).astype(jnp.int16)
        one = jnp.ones((chunk, lanes), jnp.bfloat16)
        zero = jnp.zeros((chunk, lanes), jnp.bfloat16)
        return jnp.concatenate(
            [
                jnp.where(spread_out == ladder + jnp.int16(base), one, zero)
                for base in range(0, rows, chunk)
            ],
            axis=0,
        )

    across = (((1,), (1,)), ((), ()))

    def spill(terms, picked):
        return lax.dot_general(terms, picked, across, preferred_element_type=jnp.float32)

    def begin_part(part):
        listed = pairs_ref[part]
        least = plan_ref[2 * part + 3]
        after = jnp.minimum(least + 1, image_ref.shape[0] - 1)
        pick_i = pick(atoms, listed[0:1])
        pick_j = pick(2 * width, listed[1:2] - least * width)
        pre = lower(centre_ref[...], pick_i)
        pre += lower(image_ref[least], pick_j[:width])
        pre += lower(image_ref[after], pick_j[width:])
        return pre, pick_i, pick_j

    def geometry(part, lane):
        listed = pairs_ref[part]
        extra = pre_ref[lane, hid:, :]
        sep_x = (extra[0:1] + extra[3:4]) + extra[6:7] + listed[2:3].astype(jnp.float32)
        sep_y = (extra[1:2] + extra[4:5]) + extra[7:8] + listed[3:4].astype(jnp.float32)
        sep_z = (extra[2:3] + extra[5:6]) + extra[8:9] + listed[4:5].astype(jnp.float32)
        dist_sq = sep_x * sep_x + sep_y * sep_y + sep_z * sep_z + delta_sq
        distance = jnp.sqrt(dist_sq)
        order = lax.broadcasted_iota(jnp.int32, (basis_count, lanes), 0).astype(jnp.float32)
        offset = distance - (0.25 + 0.3 * order)
        basis = jnp.exp(-(offset / spread) * (offset / spread))
        basis_high = basis.astype(jnp.bfloat16).astype(jnp.float32)
        basis_cat = jnp.concatenate(
            [basis_high, basis - basis_high, basis_high, jnp.zeros_like(basis)], axis=0
        ).astype(jnp.bfloat16)
        pre_one = pre_ref[lane, :hid, :] + lower(radial_cat_ref[...], basis_cat)
        return (sep_x, sep_y, sep_z), dist_sq, distance, offset, basis, pre_one

    def first_layer(pre_one):
        gate = 0.5 * jnp.tanh(0.5 * pre_one) + 0.5
        act = pre_one * gate
        return act.astype(jnp.bfloat16), gate + act * (1.0 - gate)

    def second_layer(pre_two, dist_sq):
        gate = 0.5 * jnp.tanh(0.5 * pre_two) + 0.5
        scaled = energy_ref[...] * gate
        scaled_act = pre_two * scaled
        readout = jnp.sum(scaled_act, axis=0, keepdims=True)
        envelope = jnp.exp(-0.5 * dist_sq)
        back = (envelope * (scaled + scaled_act * (1.0 - gate))).astype(jnp.bfloat16)
        return back, readout * envelope

    def pair_terms(part, lane, shape, back_basis, readout):
        (sep_x, sep_y, sep_z), dist_sq, distance, offset, basis, _ = shape
        weight = pairs_ref[part][5:6].astype(jnp.float32)
        extra = pre_ref[lane, hid:, :]
        charge_i = extra[9:10] + extra[10:11] + extra[11:12]
        charge_j = extra[12:13] + extra[13:14] + extra[14:15]
        inverse = 1.0 / distance
        slope_nn = (
            jnp.sum(
                back_basis * basis * (offset * (-2.0 / (spread * spread))), axis=0, keepdims=True
            )
            - readout * distance
        )
        ratio = 1.0 / (1.0 + 0.5 * distance)
        series = jnp.full_like(ratio, erfc_terms[0])
        for term in erfc_terms[1:]:
            series = series * ratio + term
        screened = ratio * jnp.exp(series - distance * distance)
        potential = screened * inverse
        slope_coul = -(2.0 / root_pi) * jnp.exp(-dist_sq) * inverse - potential * inverse
        slope = weight * (slope_nn + coulomb * charge_i * charge_j * slope_coul) * inverse
        push_x = slope * sep_x
        push_y = slope * sep_y
        push_z = slope * sep_z
        shared = weight * coulomb * potential
        terms = jnp.concatenate(
            [
                push_x,
                push_y,
                push_z,
                shared * charge_j,
                -push_x,
                -push_y,
                -push_z,
                shared * charge_i,
            ],
            axis=0,
        )
        terms_high = terms.astype(jnp.bfloat16).astype(jnp.float32)
        return jnp.concatenate([terms_high, terms - terms_high], axis=0).astype(jnp.bfloat16)

    def step(block, carry):
        parts = [block * subs + lane for lane in range(subs)]
        for lane, part in enumerate(parts):
            pre, pick_i, pick_j = begin_part(part)
            pre_ref[lane] = pre
            pick_i_ref[lane] = pick_i
            pick_j_ref[lane] = pick_j

        for lane, part in enumerate(parts):
            def gather(window, carry, lane=lane, part=part):
                entries = pairs_ref[part][1:2] - window * width
                pre_ref[lane] += lower(image_ref[window], pick(width, entries))
                return carry

            lax.fori_loop(plan_ref[2 * part + 3] + 2, plan_ref[2 * part + 4] + 1, gather, 0)

        shapes = [geometry(part, lane) for lane, part in enumerate(parts)]
        ones = [first_layer(shape[-1]) for shape in shapes]
        twos = [lower(hidden_t_ref[...], one[0]) for one in ones]
        backs = [second_layer(two, shape[1]) for two, shape in zip(twos, shapes)]
        grads = [
            (lower(hidden_ref[...], back[0]) * one[1]).astype(jnp.bfloat16)
            for back, one in zip(backs, ones)
        ]
        for lane, part in enumerate(parts):
            from_grad = lower(radial_two_ref[...], grads[lane])
            back_basis = from_grad[:basis_count] + from_grad[basis_count:]
            terms_ref[lane] = pair_terms(part, lane, shapes[lane], back_basis, backs[lane][1])
        for lane, part in enumerate(parts):
            least = plan_ref[2 * part + 3]
            after = jnp.minimum(least + 1, image_ref.shape[0] - 1)
            terms = terms_ref[lane]
            sum_i_ref[...] += spill(terms, pick_i_ref[lane])
            sum_j_ref[least] += spill(terms, pick_j_ref[lane, :width])
            sum_j_ref[after] += spill(terms, pick_j_ref[lane, width:])

        for lane, part in enumerate(parts):
            def scatter(window, carry, lane=lane, part=part):
                entries = pairs_ref[part][1:2] - window * width
                sum_j_ref[window] += spill(terms_ref[lane], pick(width, entries))
                return carry

            lax.fori_loop(plan_ref[2 * part + 3] + 2, plan_ref[2 * part + 4] + 1, scatter, 0)
        return carry

    lax.fori_loop(plan_ref[stage], plan_ref[stage + 1], step, 0)

    def finish(index, carry):
        for cut in range(cuts):
            total = sum_j_ref[index * cuts + cut]
            out_ref[index, :, cut * width : (cut + 1) * width] = total[4:8] + total[12:16]
        return carry

    lax.fori_loop(0, out_ref.shape[0], finish, 0)
    out_ref[0] += sum_i_ref[0:4, :] + sum_i_ref[8:12, :]
    if stage:
        out_ref[: before_ref.shape[0]] += before_ref[...]


def local(
    features,
    positions,
    counts,
    pair_first,
    pair_second,
    pair_mask,
    w_centre,
    w_neighbour,
    w_charge,
    w_radial,
    w_hidden,
    w_energy,
):
    own_feat = features[0, 0, 0]
    atoms, feat = own_feat.shape
    hid = w_hidden.shape[0]
    spans = [min(3, lax.axis_size(axis)) for axis in ("gx", "gy", "gz")]
    raw_charge = jnp.dot(own_feat, w_charge, preferred_element_type=jnp.float32)
    filled = counts[0, 0, 0]
    alive_slot = jnp.arange(atoms, dtype=jnp.int32) < filled
    average = jnp.sum(jnp.where(alive_slot, raw_charge, 0.0)) / filled.astype(jnp.float32)
    charges = jnp.where(alive_slot, raw_charge - average, 0.0)
    own = jnp.concatenate(
        three_parts(positions[0, 0, 0])
        + three_parts(charges[None, :])
        + [jnp.zeros((part_rows - 12, atoms), jnp.float32)],
        axis=0,
    ).astype(jnp.bfloat16)
    own = jnp.concatenate([own_feat.T, own], axis=0)

    column = jnp.stack(widen(own, "gz"))
    plane = jnp.concatenate(widen(column, "gx"))

    entry = pair_second[0, 0, 0].reshape(-1)
    slot = entry // atoms
    steps = (slot // 9 - 1, slot // 3 % 3 - 1, slot % 3 - 1)
    place = [jnp.where(step < 0, span - 1, step) for step, span in zip(steps, spans)]
    brick = (place[1] * spans[0] + place[0]) * spans[2] + place[2]
    bricks = spans[0] * spans[1] * spans[2]
    sign = ((steps[0] + 1) * 3 + steps[1] + 1) * 3 + steps[2] + 1
    key = ((brick * atoms + entry % atoms) * atoms + pair_first[0, 0, 0].reshape(-1)) * 27 + sign
    mask = pair_mask[0, 0, 0].reshape(-1) != 0
    key = jnp.where(mask, key, bricks * atoms * atoms * 27)
    key = lax.sort(key, is_stable=False)
    valid = jnp.sum(mask.astype(jnp.int32))
    lanes = 256 if key.shape[0] % (256 * subs) == 0 else 128
    width = 256 if atoms % 256 == 0 else 128
    blocks = key.shape[0] // lanes
    key = key.reshape(blocks, lanes)
    sign = key % 27
    second = key // (27 * atoms)
    rows = [
        key // 27 % atoms,
        second,
        sign // 9 - 1,
        sign // 3 % 3 - 1,
        sign % 3 - 1,
        (second < bricks * atoms).astype(jnp.int32),
    ]
    rows = rows + [jnp.zeros_like(key)] * 2
    listed = jnp.stack(rows, axis=1)
    window = jnp.minimum(second // width, bricks * atoms // width - 1)
    live = (valid + subs * lanes - 1) // (subs * lanes)
    near = spans[0] * spans[2]
    first_part = jnp.sum((second < near * atoms).astype(jnp.int32)) // (subs * lanes)
    plan = jnp.concatenate(
        [jnp.stack([jnp.zeros_like(live), first_part, live]), jnp.stack([window[:, 0], jnp.max(window, axis=1)], axis=1).reshape(-1)]
    ).astype(jnp.int32)

    carry_j = [[0.0] * part_rows for _ in range(part_rows)]
    carry_i = [[0.0] * part_rows for _ in range(part_rows)]
    for part in range(9):
        carry_j[part][part] = 1.0
        carry_i[part][part] = -1.0
    for part in range(3):
        carry_i[9 + part][9 + part] = 1.0
        carry_j[12 + part][9 + part] = 1.0

    def with_parts(weight, carried):
        top = jnp.concatenate([weight.T, jnp.zeros((hid, part_rows), jnp.bfloat16)], axis=1)
        bottom = jnp.concatenate(
            [jnp.zeros((part_rows, feat), jnp.bfloat16), jnp.array(carried, jnp.bfloat16)], axis=1
        )
        return jnp.concatenate([top, bottom], axis=0)

    radial_high = rounded(w_radial)
    radial_low = w_radial - radial_high
    radial_cat = jnp.concatenate(
        [radial_high, radial_high, radial_low, jnp.zeros_like(w_radial)], axis=0
    ).T.astype(jnp.bfloat16)
    radial_two = jnp.concatenate([radial_high, radial_low], axis=0).astype(jnp.bfloat16)

    vmem = pl.BlockSpec(memory_space=pltpu.VMEM)
    weights = [with_parts(w_centre, carry_i), with_parts(w_neighbour, carry_j)]
    weights += [radial_cat, radial_two, w_hidden, w_hidden.T, w_energy[:, None]]
    plane, listed, plan, *weights = lax.optimization_barrier((plane, listed, plan, *weights))
    tables = widen(plane, "gy")

    def run(stage, before, images, count):
        operands = [listed, *before, *images, *weights]
        windows = count * atoms // width
        pairs = key.size // (2 - stage) // 2
        return pl.pallas_call(
            functools.partial(pair_kernel, width, stage),
            out_shape=jax.ShapeDtypeStruct((count, 4, atoms), jnp.float32),
            in_specs=[pl.BlockSpec(memory_space=pltpu.SMEM)] + [vmem] * len(operands),
            out_specs=vmem,
            scratch_shapes=[
                pltpu.VMEM((hid + part_rows, atoms), jnp.bfloat16),
                pltpu.VMEM((windows, hid + part_rows, width), jnp.bfloat16),
                pltpu.VMEM((subs, hid + part_rows, lanes), jnp.float32),
                pltpu.VMEM((16, atoms), jnp.float32),
                pltpu.VMEM((windows, 16, width), jnp.float32),
                pltpu.VMEM((subs, atoms, lanes), jnp.bfloat16),
                pltpu.VMEM((subs, 2 * width, lanes), jnp.bfloat16),
                pltpu.VMEM((subs, 16, lanes), jnp.bfloat16),
            ],
            compiler_params=pltpu.CompilerParams(vmem_limit_bytes=48 * 1024 * 1024),
            cost_estimate=pl.CostEstimate(
                flops=pairs * hid * (4 * hid + 2 * atoms + 4 * width),
                bytes_accessed=count * atoms * 2 * feat,
                transcendentals=pairs * 2 * hid,
            ),
            name="near_pairs" if stage == 0 else "far_pairs",
        )(plan, *operands)

    partial = run(0, [], tables[:1], near)
    partial = run(1, [partial], tables, bricks)
    partial = partial.reshape(spans[1], spans[0], spans[2], 4, atoms)
    partial = fold(partial, "gy")
    partial = fold(partial, "gx")
    summed = fold(partial, "gz")
    return (summed[:3][None, None, None], summed[3][None, None, None])


def solution(mesh):
    placed = (
        P("gx", "gy", "gz", None, None),
        P("gx", "gy", "gz", None, None),
        P("gx", "gy", "gz"),
        P("gx", "gy", "gz", None, None),
        P("gx", "gy", "gz", None, None),
        P("gx", "gy", "gz", None, None),
        P(),
        P(),
        P(),
        P(),
        P(),
        P(),
    )
    return jax.shard_map(
        local,
        mesh=mesh,
        in_specs=placed,
        out_specs=(P("gx", "gy", "gz", None, None), P("gx", "gy", "gz", None)),
        check_vma=False,
    )
```

```python
import functools

import jax
import jax.numpy as jnp
from jax import lax
from jax.experimental import pallas as pl
from jax.experimental.pallas import tpu as pltpu
from jax.sharding import PartitionSpec as P

delta_sq = 0.04
spread = 0.3
coulomb = 0.2
root_pi = 1.7724538509055159
part_rows = 16
subs = 2
erfc_terms = (
    0.17087277,
    -0.82215223,
    1.48851587,
    -1.13520398,
    0.27886807,
    -0.18628806,
    0.09678418,
    0.37409196,
    1.00002368,
    -1.26551223,
)


def ring(axis, step):
    count = lax.axis_size(axis)
    return [(i, (i + step) % count) for i in range(count)]


def widen(block, axis):
    parts = [block, lax.ppermute(block, axis, ring(axis, -1))]
    if lax.axis_size(axis) > 2:
        parts.append(lax.ppermute(block, axis, ring(axis, 1)))
    return parts


def fold(blocks, axis):
    total = blocks[0] + lax.ppermute(blocks[1], axis, ring(axis, 1))
    if len(blocks) > 2:
        total = total + lax.ppermute(blocks[2], axis, ring(axis, -1))
    return total


def rounded(value):
    return lax.reduce_precision(value, 8, 7)


def three_parts(value):
    high = rounded(value)
    middle = rounded(value - high)
    return [high, middle, rounded(value - high - middle)]


def lower(left, right):
    return jnp.dot(left, right, preferred_element_type=jnp.float32)


def pair_kernel(
    stage,
    plan_ref,
    pairs_ref,
    *refs,
):
    before_ref = refs[0] if stage else None
    (
        *table_refs,
        project_ref,
        radial_cat_ref,
        radial_two_ref,
        hidden_ref,
        hidden_t_ref,
        energy_ref,
        out_ref,
        image_ref,
        own_ref,
        other_ref,
        sum_i_ref,
        sum_j_ref,
        pick_i_ref,
        pick_j_ref,
        terms_ref,
        copied,
    ) = refs[1:] if stage else refs
    basis_count = radial_two_ref.shape[0] // 2
    width = image_ref.shape[2]
    feat = image_ref.shape[1] - part_rows
    atoms = out_ref.shape[2]
    lanes = pairs_ref.shape[2]
    cuts = atoms // width

    copies = []
    begin = 0
    for index, table_ref in enumerate(table_refs):
        copies.append(
            pltpu.make_async_copy(
                table_ref, image_ref.at[begin : begin + table_ref.shape[0]], copied.at[index]
            )
        )
        begin += table_ref.shape[0]
    for copy in copies:
        copy.start()
    sum_i_ref[...] = jnp.zeros_like(sum_i_ref)
    sum_j_ref[...] = jnp.zeros_like(sum_j_ref)
    for copy in copies:
        copy.wait()

    chunk = 16
    ladder = lax.broadcasted_iota(jnp.int32, (chunk, lanes), 0).astype(jnp.int16)

    def pick(rows, entries):
        spread_out = jnp.broadcast_to(entries, (chunk, lanes)).astype(jnp.int16)
        one = jnp.ones((chunk, lanes), jnp.bfloat16)
        zero = jnp.zeros((chunk, lanes), jnp.bfloat16)
        return jnp.concatenate(
            [
                jnp.where(spread_out == ladder + jnp.int16(base), one, zero)
                for base in range(0, rows, chunk)
            ],
            axis=0,
        )

    across = (((1,), (1,)), ((), ()))

    def spill(terms, picked):
        return lax.dot_general(terms, picked, across, preferred_element_type=jnp.float32)

    def begin_part(part, lane):
        listed = pairs_ref[part]
        least = plan_ref[2 * part + 3]
        after = jnp.minimum(least + 1, image_ref.shape[0] - 1)
        pick_i = pick(atoms, listed[0:1])
        pick_j = pick(2 * width, listed[1:2] - least * width)
        own = lower(image_ref[0], pick_i[:width])
        for cut in range(1, cuts):
            own += lower(image_ref[cut], pick_i[cut * width : (cut + 1) * width])
        other = lower(image_ref[least], pick_j[:width])
        other += lower(image_ref[after], pick_j[width:])
        own_ref[lane] = own
        other_ref[lane] = other
        pick_i_ref[lane] = pick_i
        pick_j_ref[lane] = pick_j

    def whole(ref, lane):
        parts = ref[lane, feat:, :]
        return (parts[0:4] + parts[4:8]) + parts[8:12]

    def geometry(part, lane):
        shift = pairs_ref[part][4:8].astype(jnp.float32)
        at_i = whole(own_ref, lane)
        at_j = whole(other_ref, lane)
        sep = at_j - at_i + shift
        square = sep * sep
        dist_sq = square[0:1] + square[1:2] + square[2:3] + delta_sq
        distance = jnp.sqrt(dist_sq)
        order = lax.broadcasted_iota(jnp.int32, (basis_count, lanes), 0).astype(jnp.float32)
        offset = distance - (0.25 + 0.3 * order)
        basis = jnp.exp(-(offset / spread) * (offset / spread))
        basis_high = basis.astype(jnp.bfloat16).astype(jnp.float32)
        basis_cat = jnp.concatenate(
            [basis_high, basis - basis_high, basis_high, jnp.zeros_like(basis)], axis=0
        ).astype(jnp.bfloat16)
        both = jnp.concatenate([own_ref[lane, :feat, :], other_ref[lane, :feat, :]], axis=0)
        pre_one = lower(project_ref[...], both.astype(jnp.bfloat16))
        pre_one += lower(radial_cat_ref[...], basis_cat)
        return (at_i, at_j, sep), dist_sq, distance, offset, basis, pre_one

    def first_layer(pre_one):
        gate = 0.5 * jnp.tanh(0.5 * pre_one) + 0.5
        act = pre_one * gate
        return act.astype(jnp.bfloat16), gate + act * (1.0 - gate)

    def second_layer(pre_two, dist_sq):
        gate = 0.5 * jnp.tanh(0.5 * pre_two) + 0.5
        scaled = energy_ref[...] * gate
        scaled_act = pre_two * scaled
        readout = jnp.sum(scaled_act, axis=0, keepdims=True)
        envelope = jnp.exp(-0.5 * dist_sq)
        back = (envelope * (scaled + scaled_act * (1.0 - gate))).astype(jnp.bfloat16)
        return back, readout * envelope

    def pair_terms(part, lane, shape, back_basis, readout):
        (at_i, at_j, sep), dist_sq, distance, offset, basis, _ = shape
        weight = pairs_ref[part][2:3].astype(jnp.float32)
        charge_i = at_i[3:4]
        charge_j = at_j[3:4]
        inverse = 1.0 / distance
        slope_nn = (
            jnp.sum(
                back_basis * basis * (offset * (-2.0 / (spread * spread))), axis=0, keepdims=True
            )
            - readout * distance
        )
        ratio = 1.0 / (1.0 + 0.5 * distance)
        series = jnp.full_like(ratio, erfc_terms[0])
        for term in erfc_terms[1:]:
            series = series * ratio + term
        screened = ratio * jnp.exp(series - distance * distance)
        potential = screened * inverse
        slope_coul = -(2.0 / root_pi) * jnp.exp(-dist_sq) * inverse - potential * inverse
        slope = weight * (slope_nn + coulomb * charge_i * charge_j * slope_coul) * inverse
        push = slope * sep
        shared = weight * coulomb * potential
        last = lax.broadcasted_iota(jnp.int32, push.shape, 0) == 3
        terms = jnp.concatenate(
            [jnp.where(last, shared * at_j, push), jnp.where(last, shared * at_i, -push)], axis=0
        )
        terms_high = terms.astype(jnp.bfloat16).astype(jnp.float32)
        return jnp.concatenate([terms_high, terms - terms_high], axis=0).astype(jnp.bfloat16)

    def step(block, carry):
        parts = [block * subs + lane for lane in range(subs)]
        for lane, part in enumerate(parts):
            begin_part(part, lane)

        for lane, part in enumerate(parts):
            def gather(window, carry, lane=lane, part=part):
                entries = pairs_ref[part][1:2] - window * width
                other_ref[lane] += lower(image_ref[window], pick(width, entries))
                return carry

            lax.fori_loop(plan_ref[2 * part + 3] + 2, plan_ref[2 * part + 4] + 1, gather, 0)

        shapes = [geometry(part, lane) for lane, part in enumerate(parts)]
        ones = [first_layer(shape[-1]) for shape in shapes]
        twos = [lower(hidden_t_ref[...], one[0]) for one in ones]
        backs = [second_layer(two, shape[1]) for two, shape in zip(twos, shapes)]
        grads = [
            (lower(hidden_ref[...], back[0]) * one[1]).astype(jnp.bfloat16)
            for back, one in zip(backs, ones)
        ]
        for lane, part in enumerate(parts):
            from_grad = lower(radial_two_ref[...], grads[lane])
            back_basis = from_grad[:basis_count] + from_grad[basis_count:]
            terms_ref[lane] = pair_terms(part, lane, shapes[lane], back_basis, backs[lane][1])
        for lane, part in enumerate(parts):
            least = plan_ref[2 * part + 3]
            after = jnp.minimum(least + 1, image_ref.shape[0] - 1)
            terms = terms_ref[lane]
            sum_i_ref[...] += spill(terms, pick_i_ref[lane])
            sum_j_ref[least] += spill(terms, pick_j_ref[lane, :width])
            sum_j_ref[after] += spill(terms, pick_j_ref[lane, width:])

        for lane, part in enumerate(parts):
            def scatter(window, carry, lane=lane, part=part):
                entries = pairs_ref[part][1:2] - window * width
                sum_j_ref[window] += spill(terms_ref[lane], pick(width, entries))
                return carry

            lax.fori_loop(plan_ref[2 * part + 3] + 2, plan_ref[2 * part + 4] + 1, scatter, 0)
        return carry

    lax.fori_loop(plan_ref[stage], plan_ref[stage + 1], step, 0)

    def finish(index, carry):
        for cut in range(cuts):
            total = sum_j_ref[index * cuts + cut]
            out_ref[index, :, cut * width : (cut + 1) * width] = total[4:8] + total[12:16]
        return carry

    lax.fori_loop(0, out_ref.shape[0], finish, 0)
    out_ref[0] += sum_i_ref[0:4, :] + sum_i_ref[8:12, :]
    if stage:
        out_ref[: before_ref.shape[0]] += before_ref[...]


def local(
    features,
    positions,
    counts,
    pair_first,
    pair_second,
    pair_mask,
    w_centre,
    w_neighbour,
    w_charge,
    w_radial,
    w_hidden,
    w_energy,
):
    own_feat = features[0, 0, 0]
    atoms, feat = own_feat.shape
    hid = w_hidden.shape[0]
    spans = [min(3, lax.axis_size(axis)) for axis in ("gx", "gy", "gz")]
    raw_charge = jnp.dot(own_feat, w_charge, preferred_element_type=jnp.float32)
    filled = counts[0, 0, 0]
    alive_slot = jnp.arange(atoms, dtype=jnp.int32) < filled
    average = jnp.sum(jnp.where(alive_slot, raw_charge, 0.0)) / filled.astype(jnp.float32)
    charges = jnp.where(alive_slot, raw_charge - average, 0.0)
    own = jnp.concatenate(
        three_parts(jnp.concatenate([positions[0, 0, 0], charges[None, :]], axis=0))
        + [jnp.zeros((part_rows - 12, atoms), jnp.float32)],
        axis=0,
    ).astype(jnp.bfloat16)
    width = 256 if atoms % 256 == 0 else 128
    own = jnp.concatenate([own_feat.T, own], axis=0)
    own = jnp.stack(jnp.split(own, atoms // width, axis=1))
    column = jnp.concatenate(widen(own, "gz"))

    entry = pair_second[0, 0, 0].reshape(-1)
    slot = entry // atoms
    steps = (slot // 9 - 1, slot // 3 % 3 - 1, slot % 3 - 1)
    place = [jnp.where(step < 0, span - 1, step) for step, span in zip(steps, spans)]
    brick = (place[1] * spans[0] + place[0]) * spans[2] + place[2]
    bricks = spans[0] * spans[1] * spans[2]
    sign = ((steps[0] + 1) * 3 + steps[1] + 1) * 3 + steps[2] + 1
    key = ((brick * atoms + entry % atoms) * atoms + pair_first[0, 0, 0].reshape(-1)) * 27 + sign
    mask = pair_mask[0, 0, 0].reshape(-1) != 0
    key = jnp.where(mask, key, bricks * atoms * atoms * 27)
    key = lax.sort(key, is_stable=False)
    valid = jnp.sum(mask.astype(jnp.int32))

    column, key, w_centre, w_neighbour, w_radial, w_hidden, w_energy = lax.optimization_barrier(
        (column, key, w_centre, w_neighbour, w_radial, w_hidden, w_energy)
    )
    plane = jnp.concatenate(widen(column, "gx"))
    lanes = 256 if key.shape[0] % (256 * subs) == 0 else 128
    blocks = key.shape[0] // lanes
    key = key.reshape(blocks, lanes)
    sign = key % 27
    second = key // (27 * atoms)
    nothing = jnp.zeros_like(key)
    rows = [
        key // 27 % atoms,
        second,
        (second < bricks * atoms).astype(jnp.int32),
        nothing,
        sign // 9 - 1,
        sign // 3 % 3 - 1,
        sign % 3 - 1,
        nothing,
    ]
    listed = jnp.stack(rows, axis=1)
    window = jnp.minimum(second // width, bricks * atoms // width - 1)
    live = (valid + subs * lanes - 1) // (subs * lanes)
    near = spans[0] * spans[2]
    first_part = jnp.sum((second < near * atoms).astype(jnp.int32)) // (subs * lanes)
    plan = jnp.concatenate(
        [jnp.stack([jnp.zeros_like(live), first_part, live]), jnp.stack([window[:, 0], jnp.max(window, axis=1)], axis=1).reshape(-1)]
    ).astype(jnp.int32)

    radial_high = rounded(w_radial)
    radial_low = w_radial - radial_high
    radial_cat = jnp.concatenate(
        [radial_high, radial_high, radial_low, jnp.zeros_like(w_radial)], axis=0
    ).T.astype(jnp.bfloat16)
    radial_two = jnp.concatenate([radial_high, radial_low], axis=0).astype(jnp.bfloat16)

    vmem = pl.BlockSpec(memory_space=pltpu.VMEM)
    weights = [jnp.concatenate([w_centre, w_neighbour], axis=0).T, radial_cat, radial_two]
    weights += [w_hidden, w_hidden.T, w_energy[:, None]]
    plane, listed, plan, *weights = lax.optimization_barrier((plane, listed, plan, *weights))
    tables = widen(plane, "gy")

    def run(stage, before, images, count):
        operands = [listed, *before, *images, *weights]
        windows = count * atoms // width
        pairs = key.size // (2 - stage) // 2
        return pl.pallas_call(
            functools.partial(pair_kernel, stage),
            out_shape=jax.ShapeDtypeStruct((count, 4, atoms), jnp.float32),
            in_specs=[pl.BlockSpec(memory_space=pltpu.SMEM)]
            + [vmem] * (1 + len(before))
            + [pl.BlockSpec(memory_space=pl.ANY)] * len(images)
            + [vmem] * len(weights),
            out_specs=vmem,
            scratch_shapes=[
                pltpu.VMEM((windows, feat + part_rows, width), jnp.bfloat16),
                pltpu.VMEM((subs, feat + part_rows, lanes), jnp.float32),
                pltpu.VMEM((subs, feat + part_rows, lanes), jnp.float32),
                pltpu.VMEM((16, atoms), jnp.float32),
                pltpu.VMEM((windows, 16, width), jnp.float32),
                pltpu.VMEM((subs, atoms, lanes), jnp.bfloat16),
                pltpu.VMEM((subs, 2 * width, lanes), jnp.bfloat16),
                pltpu.VMEM((subs, 16, lanes), jnp.bfloat16),
                pltpu.SemaphoreType.DMA((len(images),)),
            ],
            compiler_params=pltpu.CompilerParams(vmem_limit_bytes=48 * 1024 * 1024),
            cost_estimate=pl.CostEstimate(
                flops=pairs * hid * (4 * hid + 2 * atoms + 4 * width),
                bytes_accessed=count * atoms * 2 * feat,
                transcendentals=pairs * 2 * hid,
            ),
            name="near_pairs" if stage == 0 else "far_pairs",
        )(plan, *operands)

    partial = run(0, [], tables[:1], near)
    partial = run(1, [partial], tables, bricks)
    partial = partial.reshape(spans[1], spans[0], spans[2], 4, atoms)
    partial = fold(partial, "gy")
    partial = fold(partial, "gx")
    summed = fold(partial, "gz")
    return (summed[:3][None, None, None], summed[3][None, None, None])


def solution(mesh):
    placed = (
        P("gx", "gy", "gz", None, None),
        P("gx", "gy", "gz", None, None),
        P("gx", "gy", "gz"),
        P("gx", "gy", "gz", None, None),
        P("gx", "gy", "gz", None, None),
        P("gx", "gy", "gz", None, None),
        P(),
        P(),
        P(),
        P(),
        P(),
        P(),
    )
    return jax.shard_map(
        local,
        mesh=mesh,
        in_specs=placed,
        out_specs=(P("gx", "gy", "gz", None, None), P("gx", "gy", "gz", None)),
        check_vma=False,
    )
```

```python
import functools

import jax
import jax.numpy as jnp
from jax import lax
from jax.experimental import pallas as pl
from jax.experimental.pallas import tpu as pltpu
from jax.sharding import PartitionSpec as P

delta_sq = 0.04
spread = 0.3
coulomb = 0.2
root_pi = 1.7724538509055159
part_rows = 16
subs = 2
erfc_terms = (
    0.17087277,
    -0.82215223,
    1.48851587,
    -1.13520398,
    0.27886807,
    -0.18628806,
    0.09678418,
    0.37409196,
    1.00002368,
    -1.26551223,
)


def ring(axis, step):
    count = lax.axis_size(axis)
    return [(i, (i + step) % count) for i in range(count)]


def widen(block, axis):
    parts = [block, lax.ppermute(block, axis, ring(axis, -1))]
    if lax.axis_size(axis) > 2:
        parts.append(lax.ppermute(block, axis, ring(axis, 1)))
    return parts


def fold(blocks, axis):
    total = blocks[0] + lax.ppermute(blocks[1], axis, ring(axis, 1))
    if len(blocks) > 2:
        total = total + lax.ppermute(blocks[2], axis, ring(axis, -1))
    return total


def rounded(value):
    return lax.reduce_precision(value, 8, 7)


def three_parts(value):
    high = rounded(value)
    middle = rounded(value - high)
    return [high, middle, rounded(value - high - middle)]


def lower(left, right):
    return jnp.dot(left, right, preferred_element_type=jnp.float32)


def pair_kernel(
    stage,
    plan_ref,
    pairs_ref,
    *refs,
):
    before_ref = refs[0] if stage else None
    (
        *table_refs,
        project_ref,
        radial_cat_ref,
        radial_two_ref,
        hidden_ref,
        hidden_t_ref,
        energy_ref,
        out_ref,
        image_ref,
        own_ref,
        other_ref,
        sum_i_ref,
        sum_j_ref,
        terms_ref,
        copied,
    ) = refs[1:] if stage else refs
    basis_count = radial_two_ref.shape[0] // 2
    width = image_ref.shape[2]
    feat = image_ref.shape[1] - part_rows
    atoms = out_ref.shape[2]
    lanes = pairs_ref.shape[2]
    cuts = atoms // width

    copies = []
    begin = 0
    for index, table_ref in enumerate(table_refs):
        copies.append(
            pltpu.make_async_copy(
                table_ref, image_ref.at[begin : begin + table_ref.shape[0]], copied.at[index]
            )
        )
        begin += table_ref.shape[0]
    for copy in copies:
        copy.start()
    sum_i_ref[...] = jnp.zeros_like(sum_i_ref)
    sum_j_ref[...] = jnp.zeros_like(sum_j_ref)
    for copy in copies:
        copy.wait()

    chunk = 16
    ladder = lax.broadcasted_iota(jnp.int32, (chunk, lanes), 0).astype(jnp.int16)

    def pick(rows, entries):
        spread_out = jnp.broadcast_to(entries, (chunk, lanes)).astype(jnp.int16)
        one = jnp.ones((chunk, lanes), jnp.bfloat16)
        zero = jnp.zeros((chunk, lanes), jnp.bfloat16)
        return jnp.concatenate(
            [
                jnp.where(spread_out == ladder + jnp.int16(base), one, zero)
                for base in range(0, rows, chunk)
            ],
            axis=0,
        )

    across = (((1,), (1,)), ((), ()))

    def spill(terms, picked):
        return lax.dot_general(terms, picked, across, preferred_element_type=jnp.float32)

    last_window = image_ref.shape[0] - 4

    def near_entries(part, turn):
        second = pairs_ref[part][1:2]
        start = plan_ref[2 * part + 3] + 4 * turn
        base = jnp.minimum(start, last_window)
        inside = (second >= start * width) & (second < (start + 4) * width)
        return base, jnp.where(inside, second - base * width, -1)

    def select(base, groups, entries):
        low = jnp.where(entries < 0, -1, entries & (2 * width - 1))
        picked = pick(2 * width, low)
        total = None
        for group in range(groups):
            table = jnp.concatenate(
                [image_ref[base + 2 * group], image_ref[base + 2 * group + 1]], axis=1
            )
            found = lower(table, picked)
            total = found if total is None else jnp.where(
                entries >= 2 * width * group, found, total
            )
        return total

    def spread_terms(terms, groups, entries):
        low = jnp.where(entries < 0, -1, entries & (width - 1))
        rows = jnp.concatenate(
            [
                jnp.where(
                    (entries >= width * group) & (entries < width * (group + 1)), terms, 0.0
                )
                for group in range(groups)
            ],
            axis=0,
        ).astype(jnp.bfloat16)
        return spill(rows, pick(width, low))

    def add_other(lane, part, turn):
        base, entries = near_entries(part, turn)
        moved = spread_terms(terms_ref[lane, 8:16, :], 4, entries)
        for group in range(4):
            sum_j_ref[base + group] += moved[8 * group : 8 * group + 8]

    def begin_part(part, lane):
        own_ref[lane] = select(0, cuts // 2, pairs_ref[part][0:1])
        base, entries = near_entries(part, 0)
        other_ref[lane] = select(base, 2, entries)

    def whole(ref, lane):
        parts = ref[lane, feat:, :]
        return (parts[0:4] + parts[4:8]) + parts[8:12]

    def geometry(part, lane):
        shift = pairs_ref[part][4:8].astype(jnp.float32)
        at_i = whole(own_ref, lane)
        at_j = whole(other_ref, lane)
        sep = at_j - at_i + shift
        square = sep * sep
        dist_sq = square[0:1] + square[1:2] + square[2:3] + delta_sq
        distance = jnp.sqrt(dist_sq)
        order = lax.broadcasted_iota(jnp.int32, (basis_count, lanes), 0).astype(jnp.float32)
        offset = distance - (0.25 + 0.3 * order)
        basis = jnp.exp(-(offset / spread) * (offset / spread))
        basis_high = basis.astype(jnp.bfloat16).astype(jnp.float32)
        basis_cat = jnp.concatenate(
            [basis_high, basis - basis_high, basis_high, jnp.zeros_like(basis)], axis=0
        ).astype(jnp.bfloat16)
        both = jnp.concatenate([own_ref[lane, :feat, :], other_ref[lane, :feat, :]], axis=0)
        pre_one = lower(project_ref[...], both.astype(jnp.bfloat16))
        pre_one += lower(radial_cat_ref[...], basis_cat)
        return (at_i, at_j, sep), dist_sq, distance, offset, basis, pre_one

    def first_layer(pre_one):
        gate = 0.5 * jnp.tanh(0.5 * pre_one) + 0.5
        act = pre_one * gate
        return act.astype(jnp.bfloat16), gate + act * (1.0 - gate)

    def second_layer(pre_two, dist_sq):
        gate = 0.5 * jnp.tanh(0.5 * pre_two) + 0.5
        scaled = energy_ref[...] * gate
        scaled_act = pre_two * scaled
        readout = jnp.sum(scaled_act, axis=0, keepdims=True)
        envelope = jnp.exp(-0.5 * dist_sq)
        back = (envelope * (scaled + scaled_act * (1.0 - gate))).astype(jnp.bfloat16)
        return back, readout * envelope

    def pair_terms(part, lane, shape, back_basis, readout):
        (at_i, at_j, sep), dist_sq, distance, offset, basis, _ = shape
        weight = pairs_ref[part][2:3].astype(jnp.float32)
        charge_i = at_i[3:4]
        charge_j = at_j[3:4]
        inverse = 1.0 / distance
        slope_nn = (
            jnp.sum(
                back_basis * basis * (offset * (-2.0 / (spread * spread))), axis=0, keepdims=True
            )
            - readout * distance
        )
        ratio = 1.0 / (1.0 + 0.5 * distance)
        series = jnp.full_like(ratio, erfc_terms[0])
        for term in erfc_terms[1:]:
            series = series * ratio + term
        screened = ratio * jnp.exp(series - distance * distance)
        potential = screened * inverse
        slope_coul = -(2.0 / root_pi) * jnp.exp(-dist_sq) * inverse - potential * inverse
        slope = weight * (slope_nn + coulomb * charge_i * charge_j * slope_coul) * inverse
        push = slope * sep
        shared = weight * coulomb * potential
        last = lax.broadcasted_iota(jnp.int32, push.shape, 0) == 3
        for_i = jnp.where(last, shared * at_j, push)
        for_j = jnp.where(last, shared * at_i, -push)
        high_i = for_i.astype(jnp.bfloat16).astype(jnp.float32)
        high_j = for_j.astype(jnp.bfloat16).astype(jnp.float32)
        return jnp.concatenate([high_i, for_i - high_i, high_j, for_j - high_j], axis=0)

    def step(block, carry):
        parts = [block * subs + lane for lane in range(subs)]
        for lane, part in enumerate(parts):
            begin_part(part, lane)

        for lane, part in enumerate(parts):
            def gather(turn, carry, lane=lane, part=part):
                base, entries = near_entries(part, turn)
                other_ref[lane] += select(base, 2, entries)
                return carry

            lax.fori_loop(1, plan_ref[2 * part + 4], gather, 0)

        shapes = [geometry(part, lane) for lane, part in enumerate(parts)]
        ones = [first_layer(shape[-1]) for shape in shapes]
        twos = [lower(hidden_t_ref[...], one[0]) for one in ones]
        backs = [second_layer(two, shape[1]) for two, shape in zip(twos, shapes)]
        grads = [
            (lower(hidden_ref[...], back[0]) * one[1]).astype(jnp.bfloat16)
            for back, one in zip(backs, ones)
        ]
        for lane, part in enumerate(parts):
            from_grad = lower(radial_two_ref[...], grads[lane])
            back_basis = from_grad[:basis_count] + from_grad[basis_count:]
            terms_ref[lane] = pair_terms(part, lane, shapes[lane], back_basis, backs[lane][1])
        for lane, part in enumerate(parts):
            sum_i_ref[...] += spread_terms(terms_ref[lane, 0:8, :], cuts, pairs_ref[part][0:1])
            add_other(lane, part, 0)

        for lane, part in enumerate(parts):
            def scatter(turn, carry, lane=lane, part=part):
                add_other(lane, part, turn)
                return carry

            lax.fori_loop(1, plan_ref[2 * part + 4], scatter, 0)
        return carry

    lax.fori_loop(plan_ref[stage], plan_ref[stage + 1], step, 0)

    def finish(index, carry):
        for cut in range(cuts):
            total = sum_j_ref[index * cuts + cut]
            out_ref[index, :, cut * width : (cut + 1) * width] = total[0:4] + total[4:8]
        return carry

    lax.fori_loop(0, out_ref.shape[0], finish, 0)
    for cut in range(cuts):
        total = sum_i_ref[8 * cut : 8 * cut + 8]
        out_ref[0, :, cut * width : (cut + 1) * width] += total[0:4] + total[4:8]
    if stage:
        out_ref[: before_ref.shape[0]] += before_ref[...]


def local(
    features,
    positions,
    counts,
    pair_first,
    pair_second,
    pair_mask,
    w_centre,
    w_neighbour,
    w_charge,
    w_radial,
    w_hidden,
    w_energy,
):
    own_feat = features[0, 0, 0]
    atoms, feat = own_feat.shape
    hid = w_hidden.shape[0]
    spans = [min(3, lax.axis_size(axis)) for axis in ("gx", "gy", "gz")]
    raw_charge = jnp.dot(own_feat, w_charge, preferred_element_type=jnp.float32)
    filled = counts[0, 0, 0]
    alive_slot = jnp.arange(atoms, dtype=jnp.int32) < filled
    average = jnp.sum(jnp.where(alive_slot, raw_charge, 0.0)) / filled.astype(jnp.float32)
    charges = jnp.where(alive_slot, raw_charge - average, 0.0)
    own = jnp.concatenate(
        three_parts(jnp.concatenate([positions[0, 0, 0], charges[None, :]], axis=0))
        + [jnp.zeros((part_rows - 12, atoms), jnp.float32)],
        axis=0,
    ).astype(jnp.bfloat16)
    width = 128
    own = jnp.concatenate([own_feat.T, own], axis=0)
    own = jnp.stack(jnp.split(own, atoms // width, axis=1))
    column = jnp.concatenate(widen(own, "gz"))

    entry = pair_second[0, 0, 0].reshape(-1)
    slot = entry // atoms
    steps = (slot // 9 - 1, slot // 3 % 3 - 1, slot % 3 - 1)
    place = [jnp.where(step < 0, span - 1, step) for step, span in zip(steps, spans)]
    brick = (place[1] * spans[0] + place[0]) * spans[2] + place[2]
    bricks = spans[0] * spans[1] * spans[2]
    sign = ((steps[0] + 1) * 3 + steps[1] + 1) * 3 + steps[2] + 1
    key = ((brick * atoms + entry % atoms) * atoms + pair_first[0, 0, 0].reshape(-1)) * 27 + sign
    mask = pair_mask[0, 0, 0].reshape(-1) != 0
    key = jnp.where(mask, key, bricks * atoms * atoms * 27)
    key = lax.sort(key, is_stable=False)
    valid = jnp.sum(mask.astype(jnp.int32))

    column, key, w_centre, w_neighbour, w_radial, w_hidden, w_energy = lax.optimization_barrier(
        (column, key, w_centre, w_neighbour, w_radial, w_hidden, w_energy)
    )
    plane = jnp.concatenate(widen(column, "gx"))
    lanes = 256 if key.shape[0] % (256 * subs) == 0 else 128
    blocks = key.shape[0] // lanes
    key = key.reshape(blocks, lanes)
    sign = key % 27
    second = key // (27 * atoms)
    nothing = jnp.zeros_like(key)
    rows = [
        key // 27 % atoms,
        second,
        (second < bricks * atoms).astype(jnp.int32),
        nothing,
        sign // 9 - 1,
        sign // 3 % 3 - 1,
        sign % 3 - 1,
        nothing,
    ]
    listed = jnp.stack(rows, axis=1)
    window = jnp.minimum(second // width, bricks * atoms // width - 1)
    near = spans[0] * spans[2]
    in_near = (second < near * atoms).astype(jnp.int32)
    live = (valid + subs * lanes - 1) // (subs * lanes)
    first_part = jnp.sum(in_near) // (subs * lanes)
    near_part = (jnp.arange(blocks) // subs) < first_part
    least = jnp.minimum(
        window[:, 0], jnp.where(near_part, near, bricks) * atoms // width - 4
    )
    turns = (jnp.max(window, axis=1) - least) // 4 + 1
    plan = jnp.concatenate(
        [jnp.stack([jnp.zeros_like(live), first_part, live]), jnp.stack([least, turns], axis=1).reshape(-1)]
    ).astype(jnp.int32)

    radial_high = rounded(w_radial)
    radial_low = w_radial - radial_high
    radial_cat = jnp.concatenate(
        [radial_high, radial_high, radial_low, jnp.zeros_like(w_radial)], axis=0
    ).T.astype(jnp.bfloat16)
    radial_two = jnp.concatenate([radial_high, radial_low], axis=0).astype(jnp.bfloat16)

    vmem = pl.BlockSpec(memory_space=pltpu.VMEM)
    weights = [jnp.concatenate([w_centre, w_neighbour], axis=0).T, radial_cat, radial_two]
    weights += [w_hidden, w_hidden.T, w_energy[:, None]]
    plane, listed, plan, *weights = lax.optimization_barrier((plane, listed, plan, *weights))
    tables = widen(plane, "gy")

    def run(stage, before, images, count):
        operands = [listed, *before, *images, *weights]
        windows = count * atoms // width
        pairs = key.size // (2 - stage) // 2
        return pl.pallas_call(
            functools.partial(pair_kernel, stage),
            out_shape=jax.ShapeDtypeStruct((count, 4, atoms), jnp.float32),
            in_specs=[pl.BlockSpec(memory_space=pltpu.SMEM)]
            + [vmem] * (1 + len(before))
            + [pl.BlockSpec(memory_space=pl.ANY)] * len(images)
            + [vmem] * len(weights),
            out_specs=vmem,
            scratch_shapes=[
                pltpu.VMEM((windows, feat + part_rows, width), jnp.bfloat16),
                pltpu.VMEM((subs, feat + part_rows, lanes), jnp.float32),
                pltpu.VMEM((subs, feat + part_rows, lanes), jnp.float32),
                pltpu.VMEM((8 * atoms // width, width), jnp.float32),
                pltpu.VMEM((windows, 8, width), jnp.float32),
                pltpu.VMEM((subs, 16, lanes), jnp.float32),
                pltpu.SemaphoreType.DMA((len(images),)),
            ],
            compiler_params=pltpu.CompilerParams(vmem_limit_bytes=48 * 1024 * 1024),
            cost_estimate=pl.CostEstimate(
                flops=pairs * hid * (4 * hid + 2 * atoms + 4 * width),
                bytes_accessed=count * atoms * 2 * feat,
                transcendentals=pairs * 2 * hid,
            ),
            name="near_pairs" if stage == 0 else "far_pairs",
        )(plan, *operands)

    partial = run(0, [], tables[:1], near)
    partial = run(1, [partial], tables, bricks)
    partial = partial.reshape(spans[1], spans[0], spans[2], 4, atoms)
    partial = fold(partial, "gy")
    partial = fold(partial, "gx")
    summed = fold(partial, "gz")
    return (summed[:3][None, None, None], summed[3][None, None, None])


def solution(mesh):
    placed = (
        P("gx", "gy", "gz", None, None),
        P("gx", "gy", "gz", None, None),
        P("gx", "gy", "gz"),
        P("gx", "gy", "gz", None, None),
        P("gx", "gy", "gz", None, None),
        P("gx", "gy", "gz", None, None),
        P(),
        P(),
        P(),
        P(),
        P(),
        P(),
    )
    return jax.shard_map(
        local,
        mesh=mesh,
        in_specs=placed,
        out_specs=(P("gx", "gy", "gz", None, None), P("gx", "gy", "gz", None)),
        check_vma=False,
    )
```

```python
import functools

import jax
import jax.numpy as jnp
from jax import lax
from jax.experimental import pallas as pl
from jax.experimental.pallas import tpu as pltpu
from jax.sharding import PartitionSpec as P

delta_sq = 0.04
spread = 0.3
coulomb = 0.2
root_pi = 1.7724538509055159
part_rows = 16
subs = 4
erfc_terms = (
    0.17087277,
    -0.82215223,
    1.48851587,
    -1.13520398,
    0.27886807,
    -0.18628806,
    0.09678418,
    0.37409196,
    1.00002368,
    -1.26551223,
)


def ring(axis, step):
    count = lax.axis_size(axis)
    return [(i, (i + step) % count) for i in range(count)]


def widen(block, axis):
    parts = [block, lax.ppermute(block, axis, ring(axis, -1))]
    if lax.axis_size(axis) > 2:
        parts.append(lax.ppermute(block, axis, ring(axis, 1)))
    return parts


def fold(blocks, axis):
    total = blocks[0] + lax.ppermute(blocks[1], axis, ring(axis, 1))
    if len(blocks) > 2:
        total = total + lax.ppermute(blocks[2], axis, ring(axis, -1))
    return total


def rounded(value):
    return lax.reduce_precision(value, 8, 7)


def three_parts(value):
    high = rounded(value)
    middle = rounded(value - high)
    return [high, middle, rounded(value - high - middle)]


def lower(left, right):
    return jnp.dot(left, right, preferred_element_type=jnp.float32)


def pair_kernel(
    stage,
    plan_ref,
    pairs_ref,
    *refs,
):
    before_ref = refs[0] if stage else None
    (
        *table_refs,
        project_ref,
        radial_cat_ref,
        radial_two_ref,
        hidden_ref,
        hidden_t_ref,
        energy_ref,
        out_ref,
        image_ref,
        own_ref,
        other_ref,
        sum_i_ref,
        sum_j_ref,
        terms_ref,
        copied,
    ) = refs[1:] if stage else refs
    basis_count = radial_two_ref.shape[0] // 2
    width = image_ref.shape[2]
    feat = image_ref.shape[1] - part_rows
    atoms = out_ref.shape[2]
    lanes = pairs_ref.shape[2]
    cuts = atoms // width

    copies = []
    begin = 0
    for index, table_ref in enumerate(table_refs):
        copies.append(
            pltpu.make_async_copy(
                table_ref, image_ref.at[begin : begin + table_ref.shape[0]], copied.at[index]
            )
        )
        begin += table_ref.shape[0]
    for copy in copies:
        copy.start()
    sum_i_ref[...] = jnp.zeros_like(sum_i_ref)
    sum_j_ref[...] = jnp.zeros_like(sum_j_ref)
    for copy in copies:
        copy.wait()

    chunk = 16
    ladder = lax.broadcasted_iota(jnp.int32, (chunk, lanes), 0).astype(jnp.int16)

    def pick(rows, entries):
        spread_out = jnp.broadcast_to(entries, (chunk, lanes)).astype(jnp.int16)
        one = jnp.ones((chunk, lanes), jnp.bfloat16)
        zero = jnp.zeros((chunk, lanes), jnp.bfloat16)
        return jnp.concatenate(
            [
                jnp.where(spread_out == ladder + jnp.int16(base), one, zero)
                for base in range(0, rows, chunk)
            ],
            axis=0,
        )

    across = (((1,), (1,)), ((), ()))

    def spill(terms, picked):
        return lax.dot_general(terms, picked, across, preferred_element_type=jnp.float32)

    last_window = image_ref.shape[0] - 4

    def near_entries(part, turn):
        second = pairs_ref[part][1:2]
        start = plan_ref[2 * part + 3] + 4 * turn
        base = jnp.minimum(start, last_window)
        inside = (second >= start * width) & (second < (start + 4) * width)
        return base, jnp.where(inside, second - base * width, -1)

    def select(base, groups, entries):
        low = jnp.where(entries < 0, -1, entries & (2 * width - 1))
        picked = pick(2 * width, low)
        total = None
        for group in range(groups):
            table = jnp.concatenate(
                [image_ref[base + 2 * group], image_ref[base + 2 * group + 1]], axis=1
            )
            found = lower(table, picked)
            total = found if total is None else jnp.where(
                entries >= 2 * width * group, found, total
            )
        return total

    def spread_terms(terms, groups, entries):
        low = jnp.where(entries < 0, -1, entries & (width - 1))
        rows = jnp.concatenate(
            [
                jnp.where(
                    (entries >= width * group) & (entries < width * (group + 1)), terms, 0.0
                )
                for group in range(groups)
            ],
            axis=0,
        ).astype(jnp.bfloat16)
        return spill(rows, pick(width, low))

    def add_other(lane, part, turn):
        base, entries = near_entries(part, turn)
        moved = spread_terms(terms_ref[lane, 8:16, :], 4, entries)
        for group in range(4):
            sum_j_ref[base + group] += moved[8 * group : 8 * group + 8]

    def begin_part(part, lane):
        own_ref[lane] = select(0, cuts // 2, pairs_ref[part][0:1])
        base, entries = near_entries(part, 0)
        other_ref[lane] = select(base, 2, entries)

    def whole(ref, lane):
        parts = ref[lane, feat:, :]
        return (parts[0:4] + parts[4:8]) + parts[8:12]

    def geometry(part, lane):
        shift = pairs_ref[part][4:8].astype(jnp.float32)
        at_i = whole(own_ref, lane)
        at_j = whole(other_ref, lane)
        sep = at_j - at_i + shift
        square = sep * sep
        dist_sq = square[0:1] + square[1:2] + square[2:3] + delta_sq
        distance = jnp.sqrt(dist_sq)
        order = lax.broadcasted_iota(jnp.int32, (basis_count, lanes), 0).astype(jnp.float32)
        offset = distance - (0.25 + 0.3 * order)
        basis = jnp.exp(-(offset / spread) * (offset / spread))
        basis_high = basis.astype(jnp.bfloat16).astype(jnp.float32)
        basis_cat = jnp.concatenate(
            [basis_high, basis - basis_high, basis_high, jnp.zeros_like(basis)], axis=0
        ).astype(jnp.bfloat16)
        both = jnp.concatenate([own_ref[lane, :feat, :], other_ref[lane, :feat, :]], axis=0)
        pre_one = lower(project_ref[...], both.astype(jnp.bfloat16))
        pre_one += lower(radial_cat_ref[...], basis_cat)
        return (at_i, at_j, sep), dist_sq, distance, offset, basis, pre_one

    def first_layer(pre_one):
        wave = jnp.tanh(pre_one)
        rise = 1.0 + wave
        act = pre_one * rise
        return act.astype(jnp.bfloat16), rise + act * (1.0 - wave)

    def second_layer(pre_two, dist_sq):
        wave = jnp.tanh(pre_two)
        scaled = energy_ref[...] * (1.0 + wave)
        scaled_act = pre_two * scaled
        readout = jnp.sum(scaled_act, axis=0, keepdims=True)
        envelope = jnp.exp(-0.5 * dist_sq)
        back = (envelope * (scaled + scaled_act * (1.0 - wave))).astype(jnp.bfloat16)
        return back, readout * envelope

    def pair_terms(part, lane, shape, back_basis, readout):
        (at_i, at_j, sep), dist_sq, distance, offset, basis, _ = shape
        weight = pairs_ref[part][2:3].astype(jnp.float32)
        charge_i = at_i[3:4]
        charge_j = at_j[3:4]
        inverse = 1.0 / distance
        slope_nn = (
            jnp.sum(
                back_basis * basis * (offset * (-2.0 / (spread * spread))), axis=0, keepdims=True
            )
            - readout * distance
        )
        ratio = 1.0 / (1.0 + 0.5 * distance)
        series = jnp.full_like(ratio, erfc_terms[0])
        for term in erfc_terms[1:]:
            series = series * ratio + term
        screened = ratio * jnp.exp(series - distance * distance)
        potential = screened * inverse
        slope_coul = -(2.0 / root_pi) * jnp.exp(-dist_sq) * inverse - potential * inverse
        slope = weight * (slope_nn + coulomb * charge_i * charge_j * slope_coul) * inverse
        push = slope * sep
        shared = weight * coulomb * potential
        last = lax.broadcasted_iota(jnp.int32, push.shape, 0) == 3
        for_i = jnp.where(last, shared * at_j, push)
        for_j = jnp.where(last, shared * at_i, -push)
        high_i = for_i.astype(jnp.bfloat16).astype(jnp.float32)
        high_j = for_j.astype(jnp.bfloat16).astype(jnp.float32)
        return jnp.concatenate([high_i, for_i - high_i, high_j, for_j - high_j], axis=0)

    def step(block, carry):
        parts = [block * subs + lane for lane in range(subs)]
        for lane, part in enumerate(parts):
            begin_part(part, lane)

        for lane, part in enumerate(parts):
            def gather(turn, carry, lane=lane, part=part):
                base, entries = near_entries(part, turn)
                other_ref[lane] += select(base, 2, entries)
                return carry

            lax.fori_loop(1, plan_ref[2 * part + 4], gather, 0)

        shapes = [geometry(part, lane) for lane, part in enumerate(parts)]
        ones = [first_layer(shape[-1]) for shape in shapes]
        twos = [lower(hidden_t_ref[...], one[0]) for one in ones]
        backs = [second_layer(two, shape[1]) for two, shape in zip(twos, shapes)]
        grads = [
            (lower(hidden_ref[...], back[0]) * one[1]).astype(jnp.bfloat16)
            for back, one in zip(backs, ones)
        ]
        for lane, part in enumerate(parts):
            from_grad = lower(radial_two_ref[...], grads[lane])
            back_basis = from_grad[:basis_count] + from_grad[basis_count:]
            terms_ref[lane] = pair_terms(part, lane, shapes[lane], back_basis, backs[lane][1])
        for lane, part in enumerate(parts):
            sum_i_ref[...] += spread_terms(terms_ref[lane, 0:8, :], cuts, pairs_ref[part][0:1])
            add_other(lane, part, 0)

        for lane, part in enumerate(parts):
            def scatter(turn, carry, lane=lane, part=part):
                add_other(lane, part, turn)
                return carry

            lax.fori_loop(1, plan_ref[2 * part + 4], scatter, 0)
        return carry

    lax.fori_loop(plan_ref[stage], plan_ref[stage + 1], step, 0)

    def finish(index, carry):
        for cut in range(cuts):
            total = sum_j_ref[index * cuts + cut]
            out_ref[index, :, cut * width : (cut + 1) * width] = total[0:4] + total[4:8]
        return carry

    lax.fori_loop(0, out_ref.shape[0], finish, 0)
    for cut in range(cuts):
        total = sum_i_ref[8 * cut : 8 * cut + 8]
        out_ref[0, :, cut * width : (cut + 1) * width] += total[0:4] + total[4:8]
    if stage:
        out_ref[: before_ref.shape[0]] += before_ref[...]


def local(
    features,
    positions,
    counts,
    pair_first,
    pair_second,
    pair_mask,
    w_centre,
    w_neighbour,
    w_charge,
    w_radial,
    w_hidden,
    w_energy,
):
    own_feat = features[0, 0, 0]
    atoms, feat = own_feat.shape
    hid = w_hidden.shape[0]
    spans = [min(3, lax.axis_size(axis)) for axis in ("gx", "gy", "gz")]
    raw_charge = jnp.dot(own_feat, w_charge, preferred_element_type=jnp.float32)
    filled = counts[0, 0, 0]
    alive_slot = jnp.arange(atoms, dtype=jnp.int32) < filled
    average = jnp.sum(jnp.where(alive_slot, raw_charge, 0.0)) / filled.astype(jnp.float32)
    charges = jnp.where(alive_slot, raw_charge - average, 0.0)
    own = jnp.concatenate(
        three_parts(jnp.concatenate([positions[0, 0, 0], charges[None, :]], axis=0))
        + [jnp.zeros((part_rows - 12, atoms), jnp.float32)],
        axis=0,
    ).astype(jnp.bfloat16)
    width = 128
    own = jnp.concatenate([own_feat.T, own], axis=0)
    own = jnp.stack(jnp.split(own, atoms // width, axis=1))
    column = jnp.concatenate(widen(own, "gz"))

    entry = pair_second[0, 0, 0].reshape(-1)
    slot = entry // atoms
    steps = (slot // 9 - 1, slot // 3 % 3 - 1, slot % 3 - 1)
    place = [jnp.where(step < 0, span - 1, step) for step, span in zip(steps, spans)]
    brick = (place[1] * spans[0] + place[0]) * spans[2] + place[2]
    bricks = spans[0] * spans[1] * spans[2]
    sign = ((steps[0] + 1) * 3 + steps[1] + 1) * 3 + steps[2] + 1
    key = ((brick * atoms + entry % atoms) * atoms + pair_first[0, 0, 0].reshape(-1)) * 27 + sign
    mask = pair_mask[0, 0, 0].reshape(-1) != 0
    key = jnp.where(mask, key, bricks * atoms * atoms * 27)
    key = lax.sort(key, is_stable=False)
    valid = jnp.sum(mask.astype(jnp.int32))
    plane = jnp.concatenate(widen(column, "gx"))
    lanes = 256 if key.shape[0] % (256 * subs) == 0 else 128
    blocks = key.shape[0] // lanes
    key = key.reshape(blocks, lanes)
    sign = key % 27
    second = key // (27 * atoms)
    nothing = jnp.zeros_like(key)
    rows = [
        key // 27 % atoms,
        second,
        (second < bricks * atoms).astype(jnp.int32),
        nothing,
        sign // 9 - 1,
        sign // 3 % 3 - 1,
        sign % 3 - 1,
        nothing,
    ]
    listed = jnp.stack(rows, axis=1)

    def whole_blocks(pairs):
        return (pairs.astype(jnp.uint32) // (subs * lanes)).astype(jnp.int32)

    window = jnp.minimum(second // width, bricks * atoms // width - 1)
    near = spans[0] * spans[2]
    in_near = (second < near * atoms).astype(jnp.int32)
    live = whole_blocks(valid + subs * lanes - 1)
    first_part = whole_blocks(jnp.sum(in_near))
    near_part = (jnp.arange(blocks) // subs) < first_part
    least = jnp.minimum(
        window[:, 0], jnp.where(near_part, near, bricks) * atoms // width - 4
    )
    turns = (jnp.max(window, axis=1) - least) // 4 + 1
    plan = jnp.concatenate(
        [jnp.stack([jnp.zeros_like(live), first_part, live]), jnp.stack([least, turns], axis=1).reshape(-1)]
    ).astype(jnp.int32)

    radial_high = rounded(w_radial)
    radial_low = w_radial - radial_high
    radial_cat = jnp.concatenate(
        [radial_high, radial_high, radial_low, jnp.zeros_like(w_radial)], axis=0
    ).T.astype(jnp.bfloat16)
    radial_two = jnp.concatenate([radial_high, radial_low], axis=0).astype(jnp.bfloat16)

    vmem = pl.BlockSpec(memory_space=pltpu.VMEM)
    half = jnp.bfloat16(0.5)
    quarter = jnp.bfloat16(0.25)
    weights = [jnp.concatenate([w_centre, w_neighbour], axis=0).T * half]
    weights += [radial_cat * half, radial_two]
    weights += [w_hidden * quarter, w_hidden.T * half, w_energy[:, None]]
    tables = widen(plane, "gy")

    def run(stage, before, images, count):
        operands = [listed, *before, *images, *weights]
        windows = count * atoms // width
        pairs = key.size // (2 - stage) // 2
        return pl.pallas_call(
            functools.partial(pair_kernel, stage),
            out_shape=jax.ShapeDtypeStruct((count, 4, atoms), jnp.float32),
            in_specs=[pl.BlockSpec(memory_space=pltpu.SMEM)]
            + [vmem] * (1 + len(before))
            + [pl.BlockSpec(memory_space=pl.ANY)] * len(images)
            + [vmem] * len(weights),
            out_specs=vmem,
            scratch_shapes=[
                pltpu.VMEM((windows, feat + part_rows, width), jnp.bfloat16),
                pltpu.VMEM((subs, feat + part_rows, lanes), jnp.float32),
                pltpu.VMEM((subs, feat + part_rows, lanes), jnp.float32),
                pltpu.VMEM((8 * atoms // width, width), jnp.float32),
                pltpu.VMEM((windows, 8, width), jnp.float32),
                pltpu.VMEM((subs, 16, lanes), jnp.float32),
                pltpu.SemaphoreType.DMA((len(images),)),
            ],
            compiler_params=pltpu.CompilerParams(vmem_limit_bytes=48 * 1024 * 1024),
            cost_estimate=pl.CostEstimate(
                flops=pairs * hid * (4 * hid + 2 * atoms + 4 * width),
                bytes_accessed=count * atoms * 2 * feat,
                transcendentals=pairs * 2 * hid,
            ),
            name="near_pairs" if stage == 0 else "far_pairs",
        )(plan, *operands)

    partial = run(0, [], tables[:1], near)
    partial = run(1, [partial], tables, bricks)
    partial = partial.reshape(spans[1], spans[0], spans[2], 4, atoms)
    partial = fold(partial, "gy")
    partial = fold(partial, "gx")
    summed = fold(partial, "gz")
    return (summed[:3][None, None, None], summed[3][None, None, None])


def solution(mesh):
    placed = (
        P("gx", "gy", "gz", None, None),
        P("gx", "gy", "gz", None, None),
        P("gx", "gy", "gz"),
        P("gx", "gy", "gz", None, None),
        P("gx", "gy", "gz", None, None),
        P("gx", "gy", "gz", None, None),
        P(),
        P(),
        P(),
        P(),
        P(),
        P(),
    )
    return jax.shard_map(
        local,
        mesh=mesh,
        in_specs=placed,
        out_specs=(P("gx", "gy", "gz", None, None), P("gx", "gy", "gz", None)),
        check_vma=False,
    )
```

```python
import functools

import jax
import jax.numpy as jnp
from jax import lax
from jax.experimental import pallas as pl
from jax.experimental.pallas import tpu as pltpu
from jax.sharding import PartitionSpec as P

delta_sq = 0.04
spread = 0.3
coulomb = 0.2
root_pi = 1.7724538509055159
part_rows = 16
subs = 4
erfc_terms = (
    0.17087277,
    -0.82215223,
    1.48851587,
    -1.13520398,
    0.27886807,
    -0.18628806,
    0.09678418,
    0.37409196,
    1.00002368,
    -1.26551223,
)


def ring(axis, step):
    count = lax.axis_size(axis)
    return [(i, (i + step) % count) for i in range(count)]


def widen(block, axis):
    parts = [block, lax.ppermute(block, axis, ring(axis, -1))]
    if lax.axis_size(axis) > 2:
        parts.append(lax.ppermute(block, axis, ring(axis, 1)))
    return parts


def fold(blocks, axis):
    total = blocks[0] + lax.ppermute(blocks[1], axis, ring(axis, 1))
    if len(blocks) > 2:
        total = total + lax.ppermute(blocks[2], axis, ring(axis, -1))
    return total


def rounded(value):
    return lax.reduce_precision(value, 8, 7)


def three_parts(value):
    high = rounded(value)
    middle = rounded(value - high)
    return [high, middle, rounded(value - high - middle)]


def lower(left, right):
    return jnp.dot(left, right, preferred_element_type=jnp.float32)


def pair_kernel(
    stage,
    plan_ref,
    pairs_ref,
    *refs,
):
    before_ref = refs[0] if stage else None
    (
        *table_refs,
        project_ref,
        radial_cat_ref,
        radial_two_ref,
        hidden_ref,
        hidden_t_ref,
        energy_ref,
        out_ref,
        image_ref,
        own_ref,
        other_ref,
        sum_i_ref,
        sum_j_ref,
        terms_ref,
        copied,
    ) = refs[1:] if stage else refs
    basis_count = radial_two_ref.shape[0] // 2
    width = image_ref.shape[2]
    feat = image_ref.shape[1] - part_rows
    atoms = out_ref.shape[2]
    lanes = pairs_ref.shape[2]
    cuts = atoms // width

    copies = []
    begin = 0
    for index, table_ref in enumerate(table_refs):
        copies.append(
            pltpu.make_async_copy(
                table_ref, image_ref.at[begin : begin + table_ref.shape[0]], copied.at[index]
            )
        )
        begin += table_ref.shape[0]
    for copy in copies:
        copy.start()
    sum_i_ref[...] = jnp.zeros_like(sum_i_ref)
    sum_j_ref[...] = jnp.zeros_like(sum_j_ref)
    for copy in copies:
        copy.wait()

    chunk = 16
    ladder = lax.broadcasted_iota(jnp.int32, (chunk, lanes), 0).astype(jnp.int16)

    def pick(rows, entries):
        spread_out = jnp.broadcast_to(entries, (chunk, lanes)).astype(jnp.int16)
        one = jnp.ones((chunk, lanes), jnp.bfloat16)
        zero = jnp.zeros((chunk, lanes), jnp.bfloat16)
        return jnp.concatenate(
            [
                jnp.where(spread_out == ladder + jnp.int16(base), one, zero)
                for base in range(0, rows, chunk)
            ],
            axis=0,
        )

    across = (((1,), (1,)), ((), ()))

    def spill(terms, picked):
        return lax.dot_general(terms, picked, across, preferred_element_type=jnp.float32)

    last_window = image_ref.shape[0] - 4

    def near_entries(part, turn):
        second = pairs_ref[part][1:2]
        start = plan_ref[2 * part + 3] + 4 * turn
        base = jnp.minimum(start, last_window)
        inside = (second >= start * width) & (second < (start + 4) * width)
        return base, jnp.where(inside, second - base * width, -1)

    def select(base, groups, entries):
        low = jnp.where(entries < 0, -1, entries & (2 * width - 1))
        picked = pick(2 * width, low)
        total = None
        for group in range(groups):
            table = jnp.concatenate(
                [image_ref[base + 2 * group], image_ref[base + 2 * group + 1]], axis=1
            )
            found = lower(table, picked)
            total = found if total is None else jnp.where(
                entries >= 2 * width * group, found, total
            )
        return total

    def spread_terms(terms, groups, entries):
        low = jnp.where(entries < 0, -1, entries & (width - 1))
        rows = jnp.concatenate(
            [
                jnp.where(
                    (entries >= width * group) & (entries < width * (group + 1)), terms, 0.0
                )
                for group in range(groups)
            ],
            axis=0,
        ).astype(jnp.bfloat16)
        return spill(rows, pick(width, low))

    def add_other(lane, part, turn):
        base, entries = near_entries(part, turn)
        moved = spread_terms(terms_ref[lane, 8:16, :], 4, entries)
        for group in range(4):
            sum_j_ref[base + group] += moved[8 * group : 8 * group + 8]

    def begin_part(part, lane):
        own_ref[lane] = select(0, cuts // 2, pairs_ref[part][0:1])
        base, entries = near_entries(part, 0)
        other_ref[lane] = select(base, 2, entries)

    def whole(ref, lane):
        parts = ref[lane, feat:, :]
        return (parts[0:4] + parts[4:8]) + parts[8:12]

    def geometry(part, lane):
        shift = pairs_ref[part][4:8].astype(jnp.float32)
        at_i = whole(own_ref, lane)
        at_j = whole(other_ref, lane)
        sep = at_j - at_i + shift
        square = sep * sep
        dist_sq = square[0:1] + square[1:2] + square[2:3] + delta_sq
        distance = jnp.sqrt(dist_sq)
        order = lax.broadcasted_iota(jnp.int32, (basis_count, lanes), 0).astype(jnp.float32)
        offset = distance - (0.25 + 0.3 * order)
        basis = jnp.exp(-(offset / spread) * (offset / spread))
        basis_high = basis.astype(jnp.bfloat16).astype(jnp.float32)
        basis_cat = jnp.concatenate(
            [basis_high, basis - basis_high, basis_high, jnp.zeros_like(basis)], axis=0
        ).astype(jnp.bfloat16)
        both = jnp.concatenate([own_ref[lane, :feat, :], other_ref[lane, :feat, :]], axis=0)
        pre_one = lower(project_ref[...], both.astype(jnp.bfloat16))
        pre_one += lower(radial_cat_ref[...], basis_cat)
        return (at_i, at_j, sep), dist_sq, distance, offset, basis, pre_one

    def first_layer(pre_one):
        wave = jnp.tanh(pre_one)
        rise = 1.0 + wave
        act = pre_one * rise
        return act.astype(jnp.bfloat16), rise + act * (1.0 - wave)

    def second_layer(pre_two, dist_sq):
        wave = jnp.tanh(pre_two)
        scaled = energy_ref[...] * (1.0 + wave)
        scaled_act = pre_two * scaled
        readout = jnp.sum(scaled_act, axis=0, keepdims=True)
        envelope = jnp.exp(-0.5 * dist_sq)
        back = (envelope * (scaled + scaled_act * (1.0 - wave))).astype(jnp.bfloat16)
        return back, readout * envelope

    def pair_terms(part, lane, shape, back_basis, readout):
        (at_i, at_j, sep), dist_sq, distance, offset, basis, _ = shape
        weight = pairs_ref[part][2:3].astype(jnp.float32)
        charge_i = at_i[3:4]
        charge_j = at_j[3:4]
        inverse = 1.0 / distance
        slope_nn = (
            jnp.sum(
                back_basis * basis * (offset * (-2.0 / (spread * spread))), axis=0, keepdims=True
            )
            - readout * distance
        )
        ratio = 1.0 / (1.0 + 0.5 * distance)
        series = jnp.full_like(ratio, erfc_terms[0])
        for term in erfc_terms[1:]:
            series = series * ratio + term
        screened = ratio * jnp.exp(series - distance * distance)
        potential = screened * inverse
        slope_coul = -(2.0 / root_pi) * jnp.exp(-dist_sq) * inverse - potential * inverse
        slope = weight * (slope_nn + coulomb * charge_i * charge_j * slope_coul) * inverse
        push = slope * sep
        shared = weight * coulomb * potential
        last = lax.broadcasted_iota(jnp.int32, push.shape, 0) == 3
        for_i = jnp.where(last, shared * at_j, push)
        for_j = jnp.where(last, shared * at_i, -push)
        high_i = for_i.astype(jnp.bfloat16).astype(jnp.float32)
        high_j = for_j.astype(jnp.bfloat16).astype(jnp.float32)
        return jnp.concatenate([high_i, for_i - high_i, high_j, for_j - high_j], axis=0)

    def step(block, carry):
        parts = [block * subs + lane for lane in range(subs)]
        for lane, part in enumerate(parts):
            begin_part(part, lane)

        for lane, part in enumerate(parts):
            def gather(turn, carry, lane=lane, part=part):
                base, entries = near_entries(part, turn)
                other_ref[lane] += select(base, 2, entries)
                return carry

            lax.fori_loop(1, plan_ref[2 * part + 4], gather, 0)

        shapes = [geometry(part, lane) for lane, part in enumerate(parts)]
        ones = [first_layer(shape[-1]) for shape in shapes]
        twos = [lower(hidden_t_ref[...], one[0]) for one in ones]
        backs = [second_layer(two, shape[1]) for two, shape in zip(twos, shapes)]
        grads = [
            (lower(hidden_ref[...], back[0]) * one[1]).astype(jnp.bfloat16)
            for back, one in zip(backs, ones)
        ]
        for lane, part in enumerate(parts):
            from_grad = lower(radial_two_ref[...], grads[lane])
            back_basis = from_grad[:basis_count] + from_grad[basis_count:]
            terms_ref[lane] = pair_terms(part, lane, shapes[lane], back_basis, backs[lane][1])
        for lane, part in enumerate(parts):
            sum_i_ref[...] += spread_terms(terms_ref[lane, 0:8, :], cuts, pairs_ref[part][0:1])
            add_other(lane, part, 0)

        for lane, part in enumerate(parts):
            def scatter(turn, carry, lane=lane, part=part):
                add_other(lane, part, turn)
                return carry

            lax.fori_loop(1, plan_ref[2 * part + 4], scatter, 0)
        return carry

    lax.fori_loop(plan_ref[stage], plan_ref[stage + 1], step, 0)

    def finish(index, carry):
        for cut in range(cuts):
            total = sum_j_ref[index * cuts + cut]
            out_ref[index, :, cut * width : (cut + 1) * width] = total[0:4] + total[4:8]
        return carry

    lax.fori_loop(0, out_ref.shape[0], finish, 0)
    for cut in range(cuts):
        total = sum_i_ref[8 * cut : 8 * cut + 8]
        out_ref[0, :, cut * width : (cut + 1) * width] += total[0:4] + total[4:8]
    if stage:
        out_ref[: before_ref.shape[0]] += before_ref[...]


def local(
    features,
    positions,
    counts,
    pair_first,
    pair_second,
    pair_mask,
    w_centre,
    w_neighbour,
    w_charge,
    w_radial,
    w_hidden,
    w_energy,
):
    own_feat = features[0, 0, 0]
    atoms, feat = own_feat.shape
    hid = w_hidden.shape[0]
    spans = [min(3, lax.axis_size(axis)) for axis in ("gx", "gy", "gz")]
    raw_charge = jnp.dot(own_feat, w_charge, preferred_element_type=jnp.float32)
    filled = counts[0, 0, 0]
    alive_slot = jnp.arange(atoms, dtype=jnp.int32) < filled
    average = jnp.sum(jnp.where(alive_slot, raw_charge, 0.0)) / filled.astype(jnp.float32)
    charges = jnp.where(alive_slot, raw_charge - average, 0.0)
    own = jnp.concatenate(
        three_parts(jnp.concatenate([positions[0, 0, 0], charges[None, :]], axis=0))
        + [jnp.zeros((part_rows - 12, atoms), jnp.float32)],
        axis=0,
    ).astype(jnp.bfloat16)
    width = 128
    own = jnp.concatenate([own_feat.T, own], axis=0)
    own = jnp.stack(jnp.split(own, atoms // width, axis=1))
    column = jnp.concatenate(widen(own, "gz"))

    entry = pair_second[0, 0, 0].reshape(-1)
    slot = entry // atoms
    steps = (slot // 9 - 1, slot // 3 % 3 - 1, slot % 3 - 1)
    place = [jnp.where(step < 0, span - 1, step) for step, span in zip(steps, spans)]
    brick = (place[1] * spans[0] + place[0]) * spans[2] + place[2]
    bricks = spans[0] * spans[1] * spans[2]
    sign = ((steps[0] + 1) * 3 + steps[1] + 1) * 3 + steps[2] + 1
    key = ((brick * atoms + entry % atoms) * atoms + pair_first[0, 0, 0].reshape(-1)) * 27 + sign
    mask = pair_mask[0, 0, 0].reshape(-1) != 0
    key = jnp.where(mask, key, bricks * atoms * atoms * 27)
    key = lax.sort(key, is_stable=False)
    valid = jnp.sum(mask.astype(jnp.int32))
    side_x = widen(column, "gx")[1:]
    side_x = jnp.concatenate(side_x) if len(side_x) > 1 else side_x[0]
    columns = widen(column, "gy")
    side_x, key = lax.optimization_barrier((side_x, key))
    lanes = 256 if key.shape[0] % (256 * subs) == 0 else 128
    blocks = key.shape[0] // lanes
    key = key.reshape(blocks, lanes)
    sign = key % 27
    second = key // (27 * atoms)
    nothing = jnp.zeros_like(key)
    rows = [
        key // 27 % atoms,
        second,
        (second < bricks * atoms).astype(jnp.int32),
        nothing,
        sign // 9 - 1,
        sign // 3 % 3 - 1,
        sign % 3 - 1,
        nothing,
    ]
    listed = jnp.stack(rows, axis=1)

    def whole_blocks(pairs):
        return (pairs.astype(jnp.uint32) // (subs * lanes)).astype(jnp.int32)

    window = jnp.minimum(second // width, bricks * atoms // width - 1)
    near = spans[0] * spans[2]
    in_near = (second < near * atoms).astype(jnp.int32)
    live = whole_blocks(valid + subs * lanes - 1)
    first_part = whole_blocks(jnp.sum(in_near))
    near_part = (jnp.arange(blocks) // subs) < first_part
    least = jnp.minimum(
        window[:, 0], jnp.where(near_part, near, bricks) * atoms // width - 4
    )
    turns = (jnp.max(window, axis=1) - least) // 4 + 1
    plan = jnp.concatenate(
        [jnp.stack([jnp.zeros_like(live), first_part, live]), jnp.stack([least, turns], axis=1).reshape(-1)]
    ).astype(jnp.int32)

    radial_high = rounded(w_radial)
    radial_low = w_radial - radial_high
    radial_cat = jnp.concatenate(
        [radial_high, radial_high, radial_low, jnp.zeros_like(w_radial)], axis=0
    ).T.astype(jnp.bfloat16)
    radial_two = jnp.concatenate([radial_high, radial_low], axis=0).astype(jnp.bfloat16)

    vmem = pl.BlockSpec(memory_space=pltpu.VMEM)
    half = jnp.bfloat16(0.5)
    quarter = jnp.bfloat16(0.25)
    weights = [jnp.concatenate([w_centre, w_neighbour], axis=0).T * half]
    weights += [radial_cat * half, radial_two]
    weights += [w_hidden * quarter, w_hidden.T * half, w_energy[:, None]]
    sides = widen(side_x, "gy")
    tables = [table for pair in zip(columns, sides) for table in pair]

    def run(stage, before, images, count):
        operands = [listed, *before, *images, *weights]
        windows = count * atoms // width
        pairs = key.size // (2 - stage) // 2
        return pl.pallas_call(
            functools.partial(pair_kernel, stage),
            out_shape=jax.ShapeDtypeStruct((count, 4, atoms), jnp.float32),
            in_specs=[pl.BlockSpec(memory_space=pltpu.SMEM)]
            + [vmem] * (1 + len(before))
            + [pl.BlockSpec(memory_space=pl.ANY)] * len(images)
            + [vmem] * len(weights),
            out_specs=vmem,
            scratch_shapes=[
                pltpu.VMEM((windows, feat + part_rows, width), jnp.bfloat16),
                pltpu.VMEM((subs, feat + part_rows, lanes), jnp.float32),
                pltpu.VMEM((subs, feat + part_rows, lanes), jnp.float32),
                pltpu.VMEM((8 * atoms // width, width), jnp.float32),
                pltpu.VMEM((windows, 8, width), jnp.float32),
                pltpu.VMEM((subs, 16, lanes), jnp.float32),
                pltpu.SemaphoreType.DMA((len(images),)),
            ],
            compiler_params=pltpu.CompilerParams(vmem_limit_bytes=48 * 1024 * 1024),
            cost_estimate=pl.CostEstimate(
                flops=pairs * hid * (4 * hid + 2 * atoms + 4 * width),
                bytes_accessed=count * atoms * 2 * feat,
                transcendentals=pairs * 2 * hid,
            ),
            name="near_pairs" if stage == 0 else "far_pairs",
        )(plan, *operands)

    partial = run(0, [], tables[:2], near)
    partial = run(1, [partial], tables, bricks)
    partial = partial.reshape(spans[1], spans[0], spans[2], 4, atoms)
    partial = fold(partial, "gy")
    partial = fold(partial, "gx")
    summed = fold(partial, "gz")
    return (summed[:3][None, None, None], summed[3][None, None, None])


def solution(mesh):
    placed = (
        P("gx", "gy", "gz", None, None),
        P("gx", "gy", "gz", None, None),
        P("gx", "gy", "gz"),
        P("gx", "gy", "gz", None, None),
        P("gx", "gy", "gz", None, None),
        P("gx", "gy", "gz", None, None),
        P(),
        P(),
        P(),
        P(),
        P(),
        P(),
    )
    return jax.shard_map(
        local,
        mesh=mesh,
        in_specs=placed,
        out_specs=(P("gx", "gy", "gz", None, None), P("gx", "gy", "gz", None)),
        check_vma=False,
    )
```
